256 devices in a mesh: tm: 16 (over y, z_lo, core), row: 4 (over x), coil: 4 (over z_hi).
Axes of the slice: x: 4, y: 4, z: 8 (z_hi: 4, z_lo: 2; z = z_hi * 2 + z_lo), core: 2. Of those that a mesh axis runs over, the one named last changes fastest.
Arguments:
- image_now: float32 [2, 16, 256, 256], P(None, 'tm', 'row'), may hold values from -6 to 6
- split_now: float32 [2, 16, 256, 256], P(None, 'tm', 'row'), may hold values from -6 to 6
- vector_one: float32 [3, 2, 16, 256, 256], P(None, None, 'tm', 'row'), may hold values from -4 to 4
- vector_two: float32 [3, 2, 16, 256, 256], P(None, None, 'tm', 'row'), may hold values from -4 to 4
- kspace_dual: float32 [2, 16, 12, 256, 256], P(None, 'tm', 'coil', 'row'), may hold values from -6 to 6
- grad_one: float32 [3, 2, 16, 256, 256], P(None, None, 'tm', 'row'), may hold values from -6 to 6
- grad_two: float32 [3, 2, 16, 256, 256], P(None, None, 'tm', 'row'), may hold values from -6 to 6
- sym_one: float32 [6, 2, 16, 256, 256], P(None, None, 'tm', 'row'), may hold values from -4 to 4
- sym_two: float32 [6, 2, 16, 256, 256], P(None, None, 'tm', 'row'), may hold values from -4 to 4
- measured: float32 [2, 16, 12, 256, 256], P(None, 'tm', 'coil', 'row'), may hold values from -6 to 6
- sensitivity: float32 [2, 12, 256, 256], P(None, 'coil', 'row'), may hold values from -4 to 4
- sampled: int32 [16, 256], P('tm'), may hold values 0 or 1
Outputs:
- image_new: float32 [2, 16, 256, 256], P(None, 'tm', 'row')
- split_new: float32 [2, 16, 256, 256], P(None, 'tm', 'row')
- vector_one_new: float32 [3, 2, 16, 256, 256], P(None, None, 'tm', 'row')
- vector_two_new: float32 [3, 2, 16, 256, 256], P(None, None, 'tm', 'row')
- kspace_new: float32 [2, 16, 12, 256, 256], P(None, 'tm', 'coil', 'row')
- grad_one_new: float32 [3, 2, 16, 256, 256], P(None, None, 'tm', 'row')
- grad_two_new: float32 [3, 2, 16, 256, 256], P(None, None, 'tm', 'row')
- sym_one_new: float32 [6, 2, 16, 256, 256], P(None, None, 'tm', 'row')
- sym_two_new: float32 [6, 2, 16, 256, 256], P(None, None, 'tm', 'row')
The draws below stay inside these ranges and needn't reach their ends.
All inputs are finite; a program needn't handle non-finite values. No bound on the sum of `sampled` on one device may be relied on, other than what follows from the above.
Results may differ from the reference program's by a relative error of at most 0.00005.
Values sent between devices are 32-bit elements; how exact they have to be, the bound alone decides.
No kernel may reach another device: no remote copies, remote signals or barrier semaphores. Data moves between devices by JAX's collectives and lax.ppermute only.
A program may use at most 64 MiB of HBM per device.

```python
import jax
import jax.numpy as jnp
from jax import lax

H = 256
W = 256
COILS = 12
FRAMES = 16


def touch_ends(array, key, smallest, largest):
    longest = array.shape.index(max(array.shape))
    spots = []
    for shift in (0, 1):
        where = [jax.random.randint(jax.random.fold_in(key, axis), (), 0, length) for axis, length in enumerate(array.shape)]
        where[longest] = (where[longest] + shift) % array.shape[longest]
        spots.append(tuple(where))
    return array.at[spots[0]].set(smallest).at[spots[1]].set(largest)


def steps_of(rng, dims, cuts, least, largest):
    def one(axis_at, blocks):
        steps = jax.random.uniform(jax.random.fold_in(jax.random.fold_in(rng, 6), axis_at), (blocks,), jnp.float32, least / len(cuts), largest / len(cuts))
        return jnp.repeat(jnp.exp(steps), dims[axis_at] // blocks).reshape((-1,) + (1,) * (len(dims) - axis_at - 1))

    level = one(*cuts[0])
    for cut in cuts[1:]:
        level = level * one(*cut)
    return level


def scatter_about(stream_key, extent, spread, reach, shards=(), dtype=jnp.bfloat16):
    drawn = jax.random.normal(stream_key, extent, jnp.float32) * spread
    if len(shards) > 0:
        drawn = steps_of(stream_key, extent, shards, -0.22, 0.18) * drawn
    return jnp.clip(drawn, min=-reach, max=reach).astype(dtype)


def setup_inputs(seed: int = 0) -> dict:
    arg_keys = jax.random.split(jax.random.key(seed), 13)
    image_now = scatter_about(arg_keys[0], (2, FRAMES, H, W), 1.0, 6.0, ((1, 16), (2, 4)), jnp.float32)
    split_now = scatter_about(arg_keys[1], (2, FRAMES, H, W), 0.5, 6.0, ((1, 16), (2, 4)), jnp.float32)
    vector_one = scatter_about(arg_keys[2], (3, 2, FRAMES, H, W), 0.3, 4.0, ((2, 16), (3, 4)), jnp.float32)
    vector_two = scatter_about(arg_keys[3], (3, 2, FRAMES, H, W), 0.3, 4.0, ((2, 16), (3, 4)), jnp.float32)
    kspace_dual = scatter_about(arg_keys[4], (2, FRAMES, COILS, W, H), 0.5, 6.0, ((1, 16), (2, 4), (3, 4)), jnp.float32)
    grad_one = scatter_about(arg_keys[5], (3, 2, FRAMES, H, W), 0.5, 6.0, ((2, 16), (3, 4)), jnp.float32)
    grad_two = scatter_about(arg_keys[6], (3, 2, FRAMES, H, W), 0.5, 6.0, ((2, 16), (3, 4)), jnp.float32)
    sym_one = scatter_about(arg_keys[7], (6, 2, FRAMES, H, W), 0.3, 4.0, ((2, 16), (3, 4)), jnp.float32)
    sym_two = scatter_about(arg_keys[8], (6, 2, FRAMES, H, W), 0.3, 4.0, ((2, 16), (3, 4)), jnp.float32)
    measured = scatter_about(arg_keys[9], (2, FRAMES, COILS, W, H), 1.0, 6.0, ((1, 16), (2, 4), (3, 4)), jnp.float32)
    sensitivity = scatter_about(arg_keys[10], (2, COILS, H, W), 0.3, 4.0, ((1, 4), (2, 4)), jnp.float32)
    sampled = touch_ends((jax.random.randint(arg_keys[11], (FRAMES, H), 0, 3) < 1).astype(jnp.int32), jax.random.fold_in(arg_keys[11], 1), 0, 1)
    return dict(image_now=image_now, split_now=split_now, vector_one=vector_one, vector_two=vector_two, kspace_dual=kspace_dual, grad_one=grad_one, grad_two=grad_two, sym_one=sym_one, sym_two=sym_two, measured=measured, sensitivity=sensitivity, sampled=sampled)


TAU = 0.25
SIGMA = 0.25
LAMBDA_DATA = 2.0
ALPHA_ONE = 2.0
ALPHA_ZERO = 1.2
BETA_ONE = 2.0
BETA_TWO = 0.5

def forward_diff(values, dimension):
    length = values.shape[dimension]
    shifted = jnp.concatenate([lax.slice_in_dim(values, 1, length, axis=dimension), lax.slice_in_dim(values, length - 1, length, axis=dimension)], axis=dimension)
    return shifted - values

def adjoint_diff(values, dimension):
    length = values.shape[dimension]
    zero_slab = jnp.zeros_like(lax.slice_in_dim(values, 0, 1, axis=dimension))
    trimmed = jnp.concatenate([lax.slice_in_dim(values, 0, length - 1, axis=dimension), zero_slab], axis=dimension)
    behind = jnp.concatenate([zero_slab, lax.slice_in_dim(trimmed, 0, length - 1, axis=dimension)], axis=dimension)
    return behind - trimmed

def gradient(values, weight):
    return jnp.stack([weight * forward_diff(values, 1), forward_diff(values, 2), forward_diff(values, 3)])

def gradient_adjoint(duals, weight):
    return weight * adjoint_diff(duals[0], 1) + adjoint_diff(duals[1], 2) + adjoint_diff(duals[2], 3)

def symmetric(vectors, weight):
    along_time = [weight * forward_diff(vectors[member], 1) for member in range(3)]
    along_rows = [forward_diff(vectors[member], 2) for member in range(3)]
    along_cols = [forward_diff(vectors[member], 3) for member in range(3)]
    return jnp.stack([along_time[0], along_rows[1], along_cols[2], 0.5 * (along_rows[0] + along_time[1]), 0.5 * (along_cols[0] + along_time[2]), 0.5 * (along_cols[1] + along_rows[2])])

def symmetric_adjoint(duals, weight):
    first_comp = weight * adjoint_diff(duals[0], 1) + 0.5 * adjoint_diff(duals[3], 2) + 0.5 * adjoint_diff(duals[4], 3)
    second_comp = adjoint_diff(duals[1], 2) + 0.5 * weight * adjoint_diff(duals[3], 1) + 0.5 * adjoint_diff(duals[5], 3)
    third_comp = adjoint_diff(duals[2], 3) + 0.5 * weight * adjoint_diff(duals[4], 1) + 0.5 * adjoint_diff(duals[5], 2)
    return jnp.stack([first_comp, second_comp, third_comp])

def project(duals, radius):
    magnitude = jnp.sqrt(lax.optimization_barrier(jnp.sum(duals * duals, axis=(0, 1))))
    return duals / jnp.maximum(1.0, magnitude / radius)[None, None]

def coil_images(image_values, sensitivity):
    sens_real = sensitivity[0][None]
    sens_imag = sensitivity[1][None]
    image_real = image_values[0][:, None]
    image_imag = image_values[1][:, None]
    return jnp.stack([sens_real * image_real - sens_imag * image_imag, sens_real * image_imag + sens_imag * image_real])

def coil_combine(coil_values, sensitivity):
    sens_real = sensitivity[0][None]
    sens_imag = sensitivity[1][None]
    real_part = lax.optimization_barrier(jnp.sum(sens_real * coil_values[0] + sens_imag * coil_values[1], axis=1))
    imag_part = lax.optimization_barrier(jnp.sum(sens_real * coil_values[1] - sens_imag * coil_values[0], axis=1))
    return jnp.stack([real_part, imag_part])

def to_kspace(coil_values):
    spectrum = jnp.fft.fft2(lax.complex(coil_values[0], coil_values[1]), norm='ortho')
    spectrum = jnp.swapaxes(spectrum, -1, -2)
    return jnp.stack([jnp.real(spectrum), jnp.imag(spectrum)])

def from_kspace(kspace_values):
    spectrum = jnp.swapaxes(lax.complex(kspace_values[0], kspace_values[1]), -1, -2)
    pictures = jnp.fft.ifft2(spectrum, norm='ortho')
    return jnp.stack([jnp.real(pictures), jnp.imag(pictures)])

def reference(image_now, split_now, vector_one, vector_two, kspace_dual, grad_one, grad_two, sym_one, sym_two, measured, sensitivity, sampled):
    mask_lines = sampled.astype(jnp.float32)[None, :, None, None, :]
    back = coil_combine(from_kspace(kspace_dual * mask_lines), sensitivity)
    tgv_one = gradient_adjoint(grad_one, BETA_ONE)
    tgv_two = gradient_adjoint(grad_two, BETA_TWO)
    image_new = image_now - TAU * (back + tgv_one)
    split_new = split_now - TAU * (tgv_two - tgv_one)
    vector_one_new = vector_one - TAU * (symmetric_adjoint(sym_one, BETA_ONE) - grad_one)
    vector_two_new = vector_two - TAU * (symmetric_adjoint(sym_two, BETA_TWO) - grad_two)
    image_bar = 2.0 * image_new - image_now
    split_bar = 2.0 * split_new - split_now
    vector_one_bar = 2.0 * vector_one_new - vector_one
    vector_two_bar = 2.0 * vector_two_new - vector_two
    predicted = to_kspace(coil_images(image_bar, sensitivity))
    kspace_new = (kspace_dual + SIGMA * mask_lines * (predicted - measured)) / (1.0 + SIGMA / LAMBDA_DATA)
    grad_one_new = project(grad_one + SIGMA * (gradient(image_bar - split_bar, BETA_ONE) - vector_one_bar), ALPHA_ONE)
    grad_two_new = project(grad_two + SIGMA * (gradient(split_bar, BETA_TWO) - vector_two_bar), ALPHA_ONE)
    sym_one_new = project(sym_one + SIGMA * symmetric(vector_one_bar, BETA_ONE), ALPHA_ZERO)
    sym_two_new = project(sym_two + SIGMA * symmetric(vector_two_bar, BETA_TWO), ALPHA_ZERO)
    return (image_new, split_new, vector_one_new, vector_two_new, kspace_new, grad_one_new, grad_two_new, sym_one_new, sym_two_new)
```

```python
import functools
import math

import jax
import jax.numpy as jnp
import ml_dtypes
import numpy as np
from jax import lax
from jax.experimental import pallas as pl
from jax.experimental.pallas import tpu as pltpu
from jax.sharding import PartitionSpec as P

TAU = 0.25
SIGMA = 0.25
LAMBDA_DATA = 2.0
ALPHA_ONE = 2.0
ALPHA_ZERO = 1.2
BETA_ONE = 2.0
BETA_TWO = 0.5

LENGTH = 256
COIL = 3
BLOCK = 64
ROWS = 4
F32 = jnp.float32
BF16 = jnp.bfloat16
LIMIT = 24 * 1024 * 1024


def dft_table():
    positions = np.arange(LENGTH)
    angles = (positions[:, None] * positions[None, :] % LENGTH) * (2.0 * math.pi / LENGTH)
    real = np.cos(angles) / math.sqrt(LENGTH)
    imag = np.sin(angles) / math.sqrt(LENGTH)
    of_real = np.concatenate([real, imag], axis=1).reshape(ROWS, 1, BLOCK, 2 * LENGTH)
    of_imag = np.concatenate([-imag, real], axis=1).reshape(ROWS, 1, BLOCK, 2 * LENGTH)
    table = np.concatenate([of_real, of_imag], axis=1).reshape(2 * LENGTH, 2 * LENGTH)
    high = table.astype(ml_dtypes.bfloat16)
    low = (table - high.astype(np.float64)).astype(ml_dtypes.bfloat16)
    return high, low


def split(values):
    high = values.astype(BF16)
    return high, (values - high.astype(F32)).astype(BF16)


def dot_nt(a, b):
    return lax.dot_general(a, b, (((1,), (1,)), ((), ())), preferred_element_type=F32)


def dot_nn(a, b):
    return lax.dot_general(a, b, (((1,), (0,)), ((), ())), preferred_element_type=F32)


def first_transform(table_high, table_low, right, row):
    def blocks(ref):
        return jnp.concatenate(
            [ref[pl.ds(pl.multiple_of(lax.rem(row + d, ROWS) * 128, 128), BLOCK), :] for d in range(ROWS)], axis=0
        )

    high, low = split(right)
    left_high = blocks(table_high)
    return dot_nt(left_high, high) + (dot_nt(left_high, low) + dot_nt(blocks(table_low), high))


def second_transform(table_high, table_low, received, row):
    def blocks(ref):
        return jnp.concatenate(
            [ref[pl.ds(pl.multiple_of(lax.rem(row + ROWS - d, ROWS) * 128, 128), 128), :] for d in range(ROWS)], axis=0
        )

    left = jnp.concatenate(
        [
            jnp.concatenate([block[:BLOCK, 128 * c : 128 * (c + 1)] for block in received], axis=1)
            for c in range(COIL)
        ],
        axis=0,
    )
    high, low = split(left)
    right_high = blocks(table_high)
    return dot_nn(high, right_high) + (dot_nn(low, right_high) + dot_nn(high, blocks(table_low)))


def iota(shape, dimension):
    return lax.broadcasted_iota(jnp.int32, shape, dimension)


ROW_PARTS = (("g1", 1), ("g2", 1), ("s1", 1), ("s1", 3), ("s1", 5), ("s2", 1), ("s2", 3), ("s2", 5))
TIME_PARTS = (("g1", 0), ("g2", 0), ("s1", 0), ("s1", 3), ("s1", 4), ("s2", 0), ("s2", 3), ("s2", 4))


def start_kernel(kd_ref, lines_ref, th_ref, tl_ref, g1_ref, g2_ref, s1_ref, s2_ref, o0, o1, o2, o3):
    row = lax.axis_index("row")
    mask = lines_ref[...].astype(F32)
    parts = []
    for c in range(COIL):
        real = kd_ref[c] * mask
        imag = kd_ref[COIL + c] * mask
        parts.append(jnp.concatenate([real, -imag], axis=1))
        parts.append(jnp.concatenate([imag, real], axis=1))
    out = first_transform(th_ref, tl_ref, jnp.concatenate(parts, axis=0), row)
    for d, ref in enumerate((o0, o1, o2, o3)):
        ref[0:BLOCK, :] = out[BLOCK * d : BLOCK * (d + 1)]
    refs = dict(g1=g1_ref, g2=g2_ref, s1=s1_ref, s2=s2_ref)
    o1[BLOCK:, LENGTH:] = jnp.zeros((16, 128), F32)
    for index, (name, part) in enumerate(ROW_PARTS):
        for reim in range(2):
            place = BLOCK + 2 * index + reim
            o1[place : place + 1, 0:LENGTH] = refs[name][2 * part + reim, 7:8, :]


def chunk(ref, plane, i):
    return ref[plane, pl.ds(pl.multiple_of(i * 8, 8), 8), :]


def plain_kernel(img, spl, v1, v2, g1, g2, s1, s2, order, q_out, w_out):
    row = lax.axis_index("row")
    keep_time = (lax.axis_index("tm") != lax.axis_size("tm") - 1).astype(F32)
    refs = dict(g1=g1, g2=g2, s1=s1, s2=s2)

    def step(i, carry):
        rows = iota((8, LENGTH), 0)
        cols = iota((8, LENGTH), 1)
        drop_row = (rows == 7) & (i == 7) & (row == ROWS - 1)

        def adj_rows(ref, plane):
            here = chunk(ref, plane, i)
            above = chunk(ref, plane, jnp.maximum(i - 1, 0))
            above = jnp.where(i == 0, 0.0, above)
            behind = jnp.where(rows == 0, pltpu.roll(above, 1, 0), pltpu.roll(here, 1, 0))
            return behind - jnp.where(drop_row, 0.0, here)

        def adj_cols(ref, plane):
            here = chunk(ref, plane, i)
            behind = jnp.where(cols == 0, 0.0, pltpu.roll(here, 1, 1))
            return behind - jnp.where(cols == LENGTH - 1, 0.0, here)

        def put(ref, plane, value):
            ref[plane, pl.ds(pl.multiple_of(i * 8, 8), 8), :] = value

        for reim in range(2):
            for index, (name, part) in enumerate(TIME_PARTS):
                put(q_out, 2 * index + reim, chunk(refs[name], 2 * part + reim, i))
            z, y, x = reim, 2 + reim, 4 + reim
            one = -BETA_ONE * keep_time * chunk(g1, z, i) + adj_rows(g1, y) + adj_cols(g1, x)
            two = -BETA_TWO * keep_time * chunk(g2, z, i) + adj_rows(g2, y) + adj_cols(g2, x)
            image = chunk(img, reim, i) - 2.0 * TAU * one
            other = chunk(spl, reim, i) - 2.0 * TAU * (two - one)
            put(w_out, reim, image - other)
            put(w_out, 2 + reim, other)
            for base, vec, grad, sym, beta in ((4, v1, g1, s1, BETA_ONE), (10, v2, g2, s2, BETA_TWO)):
                p0, p1, p2, p3, p4, p5 = (2 * k + reim for k in range(6))
                first = -beta * keep_time * chunk(sym, p0, i) + 0.5 * (adj_rows(sym, p3) + adj_cols(sym, p4))
                second = adj_rows(sym, p1) - 0.5 * beta * keep_time * chunk(sym, p3, i) + 0.5 * adj_cols(sym, p5)
                third = adj_cols(sym, p2) - 0.5 * beta * keep_time * chunk(sym, p4, i) + 0.5 * adj_rows(sym, p5)
                for k, adjoint in enumerate((first, second, third)):
                    value = chunk(vec, 2 * k + reim, i) - 2.0 * TAU * (adjoint - chunk(grad, 2 * k + reim, i))
                    put(w_out, base + 2 * k + reim, value)
        return carry

    lax.fori_loop(0, 8, step, 0)


def combine_kernel(b0, b1, b2, b3, th_ref, tl_ref, sens, out):
    row = lax.axis_index("row")
    both = second_transform(th_ref, tl_ref, (b0, b1, b2, b3), row)
    real_sum = None
    for c in range(COIL):
        real = both[BLOCK * c : BLOCK * (c + 1), :LENGTH]
        imag = both[BLOCK * c : BLOCK * (c + 1), LENGTH:]
        real_term = sens[c] * real + sens[COIL + c] * imag
        imag_term = sens[c] * imag - sens[COIL + c] * real
        real_sum = real_term if real_sum is None else real_sum + real_term
        imag_sum = imag_term if c == 0 else imag_sum + imag_term
    out[0] = real_sum
    out[1] = imag_sum


def time_term(q, field):
    if field == 0:
        return -2.0 * TAU * (2.0 * BETA_ONE * q(0) - BETA_TWO * q(1))
    if field == 1:
        return -2.0 * TAU * (BETA_TWO * q(1) - BETA_ONE * q(0))
    beta = BETA_ONE if field < 5 else BETA_TWO
    return (-2.0 * TAU * beta * (1.0 if field in (2, 5) else 0.5)) * q(field)


def row_term(r, field):
    if field == 0:
        return -2.0 * TAU * (2.0 * r(0) - r(1))
    if field == 1:
        return -2.0 * TAU * (r(1) - r(0))
    index, factor = {2: (3, 0.5), 3: (2, 1.0), 4: (4, 0.5), 5: (6, 0.5), 6: (5, 1.0), 7: (7, 0.5)}[field]
    return (-2.0 * TAU * factor) * r(index)


def predict_kernel(sum_a, sum_b, w, q_in, b1, th_ref, tl_ref, sens, o0, o1, o2, o3, z_out):
    row = lax.axis_index("row")
    rows = iota((BLOCK, LENGTH), 0)
    above = jnp.where(row == 0, 0.0, b1[BLOCK:, 0:LENGTH])
    image = []
    for reim in range(2):
        back = sum_a[reim] + sum_b[reim]
        z_out[BLOCK * reim : BLOCK * (reim + 1), :] = back
        value = w[reim] + w[2 + reim] - 2.0 * TAU * BETA_ONE * q_in[reim] - 2.0 * TAU * back
        image.append(value - 2.0 * TAU * jnp.where(rows == 0, above[reim : reim + 1], 0.0))
    z_out[2 * BLOCK :, :] = above
    parts = []
    for c in range(COIL):
        real = sens[c] * image[0] - sens[COIL + c] * image[1]
        imag = sens[c] * image[1] + sens[COIL + c] * image[0]
        parts.append(jnp.concatenate([real, imag], axis=1))
        parts.append(jnp.concatenate([-imag, real], axis=1))
    out = first_transform(th_ref, tl_ref, jnp.concatenate(parts, axis=0), row)
    for d, ref in enumerate((o0, o1, o2, o3)):
        ref[0:BLOCK, :] = out[BLOCK * d : BLOCK * (d + 1)]
    o3[BLOCK:, LENGTH:] = jnp.zeros((16, 128), F32)
    for field in range(8):
        for reim in range(2):
            plane = 2 * field + reim
            value = w[plane, 0:1, :]
            value += time_term(lambda k: q_in[2 * k + reim, 0:1, :], field)
            value += row_term(lambda k: above[2 * k + reim : 2 * k + reim + 1], field)
            if field == 0:
                value -= 2.0 * TAU * (sum_a[reim, 0:1, :] + sum_b[reim, 0:1, :])
            o3[BLOCK + plane : BLOCK + plane + 1, 0:LENGTH] = value


def finish_kernel(b0, b1, b2, b3, th_ref, tl_ref, kd_ref, measured, lines_ref, out):
    row = lax.axis_index("row")
    both = second_transform(th_ref, tl_ref, (b0, b1, b2, b3), row)
    mask = SIGMA * lines_ref[...].astype(F32)
    scale = 1.0 / (1.0 + SIGMA / LAMBDA_DATA)
    for c in range(COIL):
        real = both[BLOCK * c : BLOCK * (c + 1), :LENGTH]
        imag = -both[BLOCK * c : BLOCK * (c + 1), LENGTH:]
        out[c] = (kd_ref[c] + mask * (real - measured[c])) * scale
        out[COIL + c] = (kd_ref[COIL + c] + mask * (imag - measured[COIL + c])) * scale


def fields_kernel(
    img, spl, v1, v2, g1, g2, s1, s2, w, q_in, w_in, z, z_in, b1, n3,
    img_out, spl_out, v1_out, v2_out, g1_out, g2_out, s1_out, s2_out, bar,
):
    row = lax.axis_index("row")
    last_frame = lax.axis_index("tm") == lax.axis_size("tm") - 1
    refs = dict(g1=g1, g2=g2, s1=s1, s2=s2)
    above = jnp.where(row == 0, 0.0, b1[BLOCK:, 0:LENGTH])
    bar[:, BLOCK:, :] = jnp.zeros((16, 8, LENGTH), F32)
    for plane in range(16):
        bar[plane, BLOCK : BLOCK + 1, :] = n3[BLOCK + plane : BLOCK + plane + 1, 0:LENGTH]

    def span(i):
        return pl.ds(pl.multiple_of(i * 8, 8), 8)

    def first(i, carry):
        rows = iota((8, LENGTH), 0)
        top = (rows == 0) & (i == 0)
        for reim in range(2):
            values = []
            for field in range(8):
                plane = 2 * field + reim
                value = chunk(w, plane, i) + time_term(lambda k: chunk(q_in, 2 * k + reim, i), field)
                extra = row_term(lambda k: above[2 * k + reim : 2 * k + reim + 1], field)
                value += jnp.where(top, extra, 0.0)
                if field == 0:
                    value -= 2.0 * TAU * z[pl.ds(pl.multiple_of(BLOCK * reim + i * 8, 8), 8), :]
                bar[plane, span(i), :] = value
                values.append(value)
            img_out[reim, span(i), :] = 0.5 * (values[0] + values[1] + chunk(img, reim, i))
            spl_out[reim, span(i), :] = 0.5 * (values[1] + chunk(spl, reim, i))
            for k in range(3):
                plane = 2 * k + reim
                v1_out[plane, span(i), :] = 0.5 * (values[2 + k] + chunk(v1, plane, i))
                v2_out[plane, span(i), :] = 0.5 * (values[5 + k] + chunk(v2, plane, i))
        return carry

    lax.fori_loop(0, 8, first, 0)

    def second(i, carry):
        rows = iota((8, LENGTH), 0)
        cols = iota((8, LENGTH), 1)
        top = (rows == 0) & (i == 0)
        end_row = (rows == 7) & (i == 7) & (row == ROWS - 1)

        def along_rows(plane):
            here = chunk(bar, plane, i)
            below = chunk(bar, plane, i + 1)
            ahead = jnp.where(rows == 7, pltpu.roll(below, 7, 0), pltpu.roll(here, 7, 0))
            return jnp.where(end_row, 0.0, ahead - here)

        def along_cols(plane):
            here = chunk(bar, plane, i)
            ahead = pltpu.roll(here, LENGTH - 1, 1)
            return jnp.where(cols == LENGTH - 1, 0.0, ahead - here)

        def along_time(field, reim):
            plane = 2 * field + reim
            value = chunk(w_in, plane, i)
            value += time_term(lambda k: chunk(refs[TIME_PARTS[k][0]], 2 * TIME_PARTS[k][1] + reim, i), field)
            extra = row_term(
                lambda k: z_in[2 * BLOCK + 2 * k + reim : 2 * BLOCK + 2 * k + reim + 1, :], field
            )
            value += jnp.where(top, extra, 0.0)
            if field == 0:
                value -= 2.0 * TAU * z_in[pl.ds(pl.multiple_of(BLOCK * reim + i * 8, 8), 8), :]
            return jnp.where(last_frame, 0.0, value - chunk(bar, plane, i))

        def project(out, duals, radius):
            total = duals[0] * duals[0]
            for value in duals[1:]:
                total += value * value
            scale = 1.0 / jnp.maximum(1.0, jnp.sqrt(total) * (1.0 / radius))
            for plane, value in enumerate(duals):
                out[plane, span(i), :] = value * scale

        for dual, out, field, vec, beta in ((g1, g1_out, 0, 2, BETA_ONE), (g2, g2_out, 1, 5, BETA_TWO)):
            duals = []
            for k in range(3):
                for reim in range(2):
                    if k == 0:
                        diff = beta * along_time(field, reim)
                    else:
                        diff = (along_rows, along_cols)[k - 1](2 * field + reim)
                    diff -= chunk(bar, 2 * (vec + k) + reim, i)
                    duals.append(chunk(dual, 2 * k + reim, i) + SIGMA * diff)
            project(out, duals, ALPHA_ONE)
        for dual, out, vec, beta in ((s1, s1_out, 2, BETA_ONE), (s2, s2_out, 5, BETA_TWO)):
            duals = [None] * 12
            for reim in range(2):
                p0, p1, p2 = (2 * (vec + k) + reim for k in range(3))
                steps = (
                    beta * along_time(vec, reim),
                    along_rows(p1),
                    along_cols(p2),
                    0.5 * (along_rows(p0) + beta * along_time(vec + 1, reim)),
                    0.5 * (along_cols(p0) + beta * along_time(vec + 2, reim)),
                    0.5 * (along_cols(p1) + along_rows(p2)),
                )
                for k, diff in enumerate(steps):
                    duals[2 * k + reim] = chunk(dual, 2 * k + reim, i) + SIGMA * diff
            project(out, duals, ALPHA_ZERO)
        return carry

    lax.fori_loop(0, 8, second, 0)


def shape(*dims):
    return jax.ShapeDtypeStruct(dims, F32)


def call(kernel, outs, ins, flops, in_specs=None, scratch=(), grid=()):
    size = sum(math.prod(x.shape) * x.dtype.itemsize for x in (*ins, *outs))
    return pl.pallas_call(
        kernel,
        out_shape=outs,
        grid=grid,
        in_specs=in_specs or [pl.BlockSpec(memory_space=pltpu.VMEM)] * len(ins),
        out_specs=[pl.BlockSpec(memory_space=pltpu.VMEM)] * len(outs),
        scratch_shapes=list(scratch),
        compiler_params=pltpu.CompilerParams(vmem_limit_bytes=LIMIT),
        cost_estimate=pl.CostEstimate(flops=flops, bytes_accessed=size, transcendentals=0),
    )(*ins)


def turn(block, distance):
    return lax.ppermute(block, "row", [(i, (i + distance) % ROWS) for i in range(ROWS)])


def body(
    image_now, split_now, vector_one, vector_two, kspace_dual, grad_one, grad_two, sym_one, sym_two,
    measured, sensitivity, sampled,
):
    planes = lambda x: x.reshape(-1, BLOCK, LENGTH)
    img, spl, v1, v2, kd = map(planes, (image_now, split_now, vector_one, vector_two, kspace_dual))
    g1, g2, s1, s2, meas, sens = map(planes, (grad_one, grad_two, sym_one, sym_two, measured, sensitivity))
    high, low = map(jnp.asarray, dft_table())
    frames = lax.axis_size("tm")
    vmem = pl.BlockSpec(memory_space=pltpu.VMEM)
    blocks = (shape(BLOCK, 384), shape(BLOCK + 16, 384), shape(BLOCK, 384), shape(BLOCK, 384))

    def bottom(x):
        return pl.BlockSpec((x.shape[0], 8, LENGTH), lambda _: (0, BLOCK // 8 - 1, 0))

    a0, a1, a2, a3 = call(
        start_kernel, blocks, (kd, sampled, high, low, g1, g2, s1, s2), 6 * 256 * 512 * 384,
        in_specs=[vmem] * 4 + [bottom(x) for x in (g1, g2, s1, s2)], grid=(1,),
    )
    b1, b2, b3 = turn(a1, 1), turn(a2, 2), turn(a3, 3)
    q_out, w_out = call(
        plain_kernel, (shape(16, BLOCK, LENGTH), shape(16, BLOCK, LENGTH)),
        (img, spl, v1, v2, g1, g2, s1, s2, a0), 16 * 30 * BLOCK * LENGTH,
        in_specs=[vmem] * 8 + [pl.BlockSpec(memory_space=pl.ANY)],
    )
    q_in = lax.ppermute(q_out, "tm", [(i, i + 1) for i in range(frames - 1)])
    pairs = []
    groups = lax.axis_size("coil")
    for t in range(1, frames):
        for c in range(groups):
            to = c if t % 2 else ((c + 1) % groups if t % 4 == 2 else (c - 1) % groups)
            pairs.append((t * groups + c, (t - 1) * groups + to))
    w_in = lax.ppermute(w_out, ("tm", "coil"), pairs)
    (partial,) = call(
        combine_kernel, (shape(2, BLOCK, LENGTH),), (a0, b1, b2, b3, high, low, sens), 6 * 192 * 512 * 512
    )
    pair = partial + lax.ppermute(partial, "coil", [(0, 1), (1, 0), (2, 3), (3, 2)])
    rest = lax.ppermute(pair, "coil", [(0, 3), (3, 0), (1, 2), (2, 1)])
    c_blocks = (shape(BLOCK, 384), shape(BLOCK, 384), shape(BLOCK, 384), shape(BLOCK + 16, 384))
    c0, c1, c2, c3, z = call(
        predict_kernel, (*c_blocks, shape(2 * BLOCK + 16, LENGTH)),
        (pair, rest, w_out, q_in, b1, high, low, sens), 6 * 256 * 512 * 384,
    )
    n3, n1, n2 = turn(c3, 3), turn(c1, 1), turn(c2, 2)
    z_in = lax.ppermute(z, "tm", [(i + 1, i) for i in range(frames - 1)])
    like = lambda x: shape(*x.shape)
    fields = call(
        fields_kernel, tuple(map(like, (img, spl, v1, v2, g1, g2, s1, s2))),
        (img, spl, v1, v2, g1, g2, s1, s2, w_out, q_in, w_in, z, z_in, b1, n3), 16 * 60 * BLOCK * LENGTH,
        scratch=[pltpu.VMEM((16, BLOCK + 8, LENGTH), F32)],
    )
    (kspace,) = call(
        finish_kernel, (like(kd),), (c0, n1, n2, n3, high, low, kd, meas, sampled), 6 * 192 * 512 * 512
    )
    img_new, spl_new, v1_new, v2_new, g1_new, g2_new, s1_new, s2_new = fields
    news = (img_new, spl_new, v1_new, v2_new, kspace, g1_new, g2_new, s1_new, s2_new)
    olds = (image_now, split_now, vector_one, vector_two, kspace_dual, grad_one, grad_two, sym_one, sym_two)
    return tuple(new.reshape(old.shape) for new, old in zip(news, olds))


def solution(mesh):
    image = P(None, "tm", "row", None)
    vector = P(None, None, "tm", "row", None)
    kspace = P(None, "tm", "coil", "row", None)
    return jax.shard_map(
        body,
        mesh=mesh,
        in_specs=(
            image, image, vector, vector, kspace, vector, vector, vector, vector, kspace,
            P(None, "coil", "row", None), P("tm", None),
        ),
        out_specs=(image, image, vector, vector, kspace, vector, vector, vector, vector),
        check_vma=False,
    )
```

```python
import functools
import math

import jax
import jax.numpy as jnp
import ml_dtypes
import numpy as np
from jax import lax
from jax.experimental import pallas as pl
from jax.experimental.pallas import tpu as pltpu
from jax.sharding import PartitionSpec as P

TAU = 0.25
SIGMA = 0.25
LAMBDA_DATA = 2.0
ALPHA_ONE = 2.0
ALPHA_ZERO = 1.2
BETA_ONE = 2.0
BETA_TWO = 0.5

LENGTH = 256
COIL = 3
BLOCK = 64
ROWS = 4
F32 = jnp.float32
BF16 = jnp.bfloat16
LIMIT = 12 * 1024 * 1024


def halves(table):
    high = table.astype(ml_dtypes.bfloat16)
    return high, (table - high.astype(np.float64)).astype(ml_dtypes.bfloat16)


def dft_tables():
    positions = np.arange(LENGTH)
    angles = (positions[:, None] * positions[None, :] % LENGTH) * (2.0 * math.pi / LENGTH)
    real = np.cos(angles) / math.sqrt(LENGTH)
    imag = np.sin(angles) / math.sqrt(LENGTH)
    of_real = np.concatenate([real, imag], axis=1).reshape(ROWS, 1, BLOCK, 2 * LENGTH)
    of_imag = np.concatenate([-imag, real], axis=1).reshape(ROWS, 1, BLOCK, 2 * LENGTH)
    table = np.concatenate([of_real, of_imag], axis=1).reshape(2 * LENGTH, 2 * LENGTH)
    return halves(of_real.reshape(LENGTH, 2 * LENGTH)) + halves(table)


def split(values):
    high = values.astype(BF16)
    return high, (values - high.astype(F32)).astype(BF16)


def dot_nt(a, b):
    return lax.dot_general(a, b, (((1,), (1,)), ((), ())), preferred_element_type=F32)


def dot_nn(a, b):
    return lax.dot_general(a, b, (((1,), (0,)), ((), ())), preferred_element_type=F32)


def first_transform(table_high, table_low, right, row):
    def blocks(ref):
        return jnp.concatenate(
            [ref[pl.ds(pl.multiple_of(lax.rem(row + d, ROWS) * BLOCK, BLOCK), BLOCK), :] for d in range(ROWS)], axis=0
        )

    high, low = split(right)
    left_high = blocks(table_high)
    return dot_nt(left_high, high) + (dot_nt(left_high, low) + dot_nt(blocks(table_low), high))


def second_transform(table_high, table_low, received, row):
    def blocks(ref):
        return jnp.concatenate(
            [ref[pl.ds(pl.multiple_of(lax.rem(row + ROWS - d, ROWS) * 128, 128), 128), :] for d in range(ROWS)], axis=0
        )

    left = jnp.concatenate(
        [
            jnp.concatenate([block[:BLOCK, 128 * c : 128 * (c + 1)] for block in received], axis=1)
            for c in range(COIL)
        ],
        axis=0,
    )
    high, low = split(left)
    right_high = blocks(table_high)
    return dot_nn(high, right_high) + (dot_nn(low, right_high) + dot_nn(high, blocks(table_low)))


def iota(shape, dimension):
    return lax.broadcasted_iota(jnp.int32, shape, dimension)


ROW_PARTS = (("g1", 1), ("g2", 1), ("s1", 1), ("s1", 3), ("s1", 5), ("s2", 1), ("s2", 3), ("s2", 5))
TIME_PARTS = (("g1", 0), ("g2", 0), ("s1", 0), ("s1", 3), ("s1", 4), ("s2", 0), ("s2", 3), ("s2", 4))


def start_kernel(
    kd_hbm, lines_hbm, th_hbm, tl_hbm, g1, g2, s1, s2, o0, o1, o2, o3,
    kd_ref, lines_ref, th_ref, tl_ref, ends, sems
):
    row = lax.axis_index("row")
    copies = [
        pltpu.make_async_copy(source, target, sems.at[k])
        for k, (source, target) in enumerate(
            ((kd_hbm, kd_ref), (lines_hbm, lines_ref), (th_hbm, th_ref), (tl_hbm, tl_ref))
        )
    ]
    refs = dict(g1=g1, g2=g2, s1=s1, s2=s2)
    for index, (name, part) in enumerate(ROW_PARTS):
        copies.append(
            pltpu.make_async_copy(
                refs[name].at[2 * part : 2 * part + 2, BLOCK - 8 : BLOCK, :],
                ends.at[2 * index : 2 * index + 2],
                sems.at[4 + index],
            )
        )
    for copy in copies:
        copy.start()
    for copy in copies[:4]:
        copy.wait()
    mask = lines_ref[...].astype(F32)
    parts = []
    for c in range(COIL):
        real = kd_ref[c] * mask
        imag = kd_ref[COIL + c] * mask
        parts.append(jnp.concatenate([real, -imag], axis=1))
        parts.append(jnp.concatenate([imag, real], axis=1))
    out = first_transform(th_ref, tl_ref, jnp.concatenate(parts, axis=0), row)
    for d, ref in enumerate((o0, o1, o2, o3)):
        ref[0:BLOCK, :] = out[BLOCK * d : BLOCK * (d + 1)]
    for copy in copies[4:]:
        copy.wait()
    o1[BLOCK:, LENGTH:] = jnp.zeros((16, 128), F32)
    for plane in range(16):
        o1[BLOCK + plane : BLOCK + plane + 1, 0:LENGTH] = ends[plane, 7:8, :]


def chunk(ref, plane, i):
    return ref[plane, pl.ds(i * 8 if isinstance(i, int) else pl.multiple_of(i * 8, 8), 8), :]


def pack_kernel(g1, g2, s1, s2, order, q_first, q_out):
    refs = dict(g1=g1, g2=g2, s1=s1, s2=s2)
    for reim in range(2):
        q_first[BLOCK * reim : BLOCK * (reim + 1), :] = g1[reim]
        tops = [refs[name][2 * part + reim, 0:1, :] for name, part in TIME_PARTS]
        for field in range(8):
            place = 2 * BLOCK + 2 * field + reim
            q_first[place : place + 1, :] = time_term(lambda k: tops[k], field)
        for index, (name, part) in enumerate(TIME_PARTS[1:]):
            q_out[2 * index + reim] = refs[name][2 * part + reim]


def plain_kernel(img, spl, v1, v2, g1, g2, s1, s2, b1, order, w_out, w_top):
    row = lax.axis_index("row")
    keep_time = (lax.axis_index("tm") != lax.axis_size("tm") - 1).astype(F32)
    refs = dict(g1=g1, g2=g2, s1=s1, s2=s2)
    edge = jnp.where(row == 0, 0.0, b1[BLOCK:, 0:LENGTH])
    where = {part: 2 * index for index, part in enumerate(ROW_PARTS)}

    def step(i, carry):
        rows = iota((8, LENGTH), 0)
        cols = iota((8, LENGTH), 1)
        drop_row = (rows == 7) & (i == 7) & (row == ROWS - 1)

        def adj_rows(name, plane):
            ref = refs[name]
            here = chunk(ref, plane, i)
            above = chunk(ref, plane, jnp.maximum(i - 1, 0))
            at = where[name, plane // 2] + plane % 2
            above = jnp.where(i == 0, edge[at : at + 1], above)
            behind = jnp.where(rows == 0, pltpu.roll(above, 1, 0), pltpu.roll(here, 1, 0))
            return behind - jnp.where(drop_row, 0.0, here)

        def adj_cols(ref, plane):
            here = chunk(ref, plane, i)
            behind = jnp.where(cols == 0, 0.0, pltpu.roll(here, 1, 1))
            return behind - jnp.where(cols == LENGTH - 1, 0.0, here)

        def put(ref, plane, value):
            ref[plane, pl.ds(pl.multiple_of(i * 8, 8), 8), :] = value

        for reim in range(2):
            z, y, x = reim, 2 + reim, 4 + reim
            one = -BETA_ONE * keep_time * chunk(g1, z, i) + adj_rows("g1", y) + adj_cols(g1, x)
            two = -BETA_TWO * keep_time * chunk(g2, z, i) + adj_rows("g2", y) + adj_cols(g2, x)
            image = chunk(img, reim, i) - 2.0 * TAU * one
            other = chunk(spl, reim, i) - 2.0 * TAU * (two - one)
            put(w_out, reim, image - other)
            put(w_out, 2 + reim, other)
            for base, vec, grad, name, beta in ((4, v1, g1, "s1", BETA_ONE), (10, v2, g2, "s2", BETA_TWO)):
                sym = refs[name]
                p0, p1, p2, p3, p4, p5 = (2 * k + reim for k in range(6))
                first = -beta * keep_time * chunk(sym, p0, i) + 0.5 * (adj_rows(name, p3) + adj_cols(sym, p4))
                second = adj_rows(name, p1) - 0.5 * beta * keep_time * chunk(sym, p3, i) + 0.5 * adj_cols(sym, p5)
                third = adj_cols(sym, p2) - 0.5 * beta * keep_time * chunk(sym, p4, i) + 0.5 * adj_rows(name, p5)
                for k, adjoint in enumerate((first, second, third)):
                    value = chunk(vec, 2 * k + reim, i) - 2.0 * TAU * (adjoint - chunk(grad, 2 * k + reim, i))
                    put(w_out, base + 2 * k + reim, value)
        return carry

    lax.fori_loop(0, 8, step, 0)
    for plane in range(16):
        w_top[plane : plane + 1, :] = w_out[plane, 0:1, :]


def combine_kernel(b0, b1, b2, b3, th_ref, tl_ref, sens, out):
    row = lax.axis_index("row")
    both = second_transform(th_ref, tl_ref, (b0, b1, b2, b3), row)
    real_sum = None
    for c in range(COIL):
        real = both[BLOCK * c : BLOCK * (c + 1), :LENGTH]
        imag = both[BLOCK * c : BLOCK * (c + 1), LENGTH:]
        real_term = sens[c] * real + sens[COIL + c] * imag
        imag_term = sens[c] * imag - sens[COIL + c] * real
        real_sum = real_term if real_sum is None else real_sum + real_term
        imag_sum = imag_term if c == 0 else imag_sum + imag_term
    out[0] = real_sum
    out[1] = imag_sum


def time_term(q, field):
    if field == 0:
        return -2.0 * TAU * (2.0 * BETA_ONE * q(0) - BETA_TWO * q(1))
    if field == 1:
        return -2.0 * TAU * (BETA_TWO * q(1) - BETA_ONE * q(0))
    beta = BETA_ONE if field < 5 else BETA_TWO
    return (-2.0 * TAU * beta * (1.0 if field in (2, 5) else 0.5)) * q(field)


def predict_kernel(sum_a, sum_b, w, w_top, q_first, th_ref, tl_ref, sens, o0, o1, o2, o3, z_out, q0_out):
    row = lax.axis_index("row")
    image = []
    for reim in range(2):
        back = sum_a[reim] + sum_b[reim]
        z_out[reim] = back
        before = q_first[BLOCK * reim : BLOCK * (reim + 1), :]
        q0_out[reim] = before
        image.append(w[reim] + w[2 + reim] - 2.0 * TAU * BETA_ONE * before - 2.0 * TAU * back)
    parts = []
    for c in range(COIL):
        real = sens[c] * image[0] - sens[COIL + c] * image[1]
        imag = sens[c] * image[1] + sens[COIL + c] * image[0]
        parts.append(jnp.concatenate([real, imag], axis=1))
        parts.append(jnp.concatenate([-imag, real], axis=1))
    out = first_transform(th_ref, tl_ref, jnp.concatenate(parts, axis=0), row)
    for d, ref in enumerate((o0, o1, o2, o3)):
        ref[0:BLOCK, :] = out[BLOCK * d : BLOCK * (d + 1)]
    o3[BLOCK:, LENGTH:] = jnp.zeros((16, 128), F32)
    o3[BLOCK:, 0:LENGTH] = w_top[...] + q_first[2 * BLOCK :, :]
    for reim in range(2):
        o3[BLOCK + reim : BLOCK + reim + 1, 0:LENGTH] -= 2.0 * TAU * (sum_a[reim, 0:1, :] + sum_b[reim, 0:1, :])


def finish_kernel(b0, b1, b2, b3, th_ref, tl_ref, kd_ref, measured, lines_hbm, out_hbm, lines_ref, out, sems):
    row = lax.axis_index("row")
    lines = pltpu.make_async_copy(lines_hbm, lines_ref, sems.at[0])
    lines.start()
    both = second_transform(th_ref, tl_ref, (b0, b1, b2, b3), row)
    lines.wait()
    mask = SIGMA * lines_ref[...].astype(F32)
    scale = 1.0 / (1.0 + SIGMA / LAMBDA_DATA)
    copies = []
    for c in range(COIL):
        real = both[BLOCK * c : BLOCK * (c + 1), :LENGTH]
        imag = -both[BLOCK * c : BLOCK * (c + 1), LENGTH:]
        for plane, value in ((c, real), (COIL + c, imag)):
            out[plane] = (kd_ref[plane] + mask * (value - measured[plane])) * scale
            copies.append(pltpu.make_async_copy(out.at[plane], out_hbm.at[plane], sems.at[1 + plane]))
            copies[-1].start()
    for copy in copies:
        copy.wait()


def fields_kernel(
    img, spl, v1, v2, g1, g2, s1, s2, w, q0, q_in, w_in, z, z_in, n3,
    img_hbm, spl_hbm, v1_hbm, v2_hbm, g1_hbm, g2_hbm, s1_hbm, s2_hbm,
    bar, img_out, spl_out, v1_out, v2_out, g1_out, g2_out, s1_out, s2_out, sems,
):
    row = lax.axis_index("row")
    keep_time = (lax.axis_index("tm") != lax.axis_size("tm") - 1).astype(F32)
    refs = dict(g1=g1, g2=g2, s1=s1, s2=s2)
    copies = [
        pltpu.make_async_copy(source, target, sems.at[k])
        for k, (source, target) in enumerate(
            ((img_out, img_hbm), (spl_out, spl_hbm), (v1_out, v1_hbm), (v2_out, v2_hbm))
        )
    ]

    def span(i):
        return pl.ds(i * 8 if isinstance(i, int) else pl.multiple_of(i * 8, 8), 8)

    def first(i, carry):
        for reim in range(2):

            def before(k):
                if k == 0:
                    return chunk(q0, reim, i)
                return chunk(q_in, 2 * (k - 1) + reim, i)

            values = []
            for field in range(8):
                plane = 2 * field + reim
                value = chunk(w, plane, i) + time_term(before, field)
                if field == 0:
                    value -= 2.0 * TAU * chunk(z, reim, i)
                bar[plane, span(i), :] = value
                values.append(value)
            img_out[reim, span(i), :] = 0.5 * (values[0] + values[1] + chunk(img, reim, i))
            spl_out[reim, span(i), :] = 0.5 * (values[1] + chunk(spl, reim, i))
            for k in range(3):
                plane = 2 * k + reim
                v1_out[plane, span(i), :] = 0.5 * (values[2 + k] + chunk(v1, plane, i))
                v2_out[plane, span(i), :] = 0.5 * (values[5 + k] + chunk(v2, plane, i))
        return carry

    lax.fori_loop(0, 8, first, 0, unroll=2)
    for copy in copies:
        copy.start()
    for plane in range(16):
        below = n3[BLOCK + plane : BLOCK + plane + 1, 0:LENGTH]
        bar[plane, BLOCK : BLOCK + 1, :] = jnp.where(row == ROWS - 1, bar[plane, BLOCK - 1 : BLOCK, :], below)

    def along_rows(plane, i):
        here = chunk(bar, plane, i)
        below = chunk(bar, plane, i + 1)
        rows = iota((8, LENGTH), 0)
        return jnp.where(rows == 7, pltpu.roll(below, 7, 0), pltpu.roll(here, 7, 0)) - here

    def along_cols(plane, i):
        here = chunk(bar, plane, i)
        cols = iota((8, LENGTH), 1)
        return jnp.where(cols == LENGTH - 1, 0.0, pltpu.roll(here, LENGTH - 1, 1) - here)

    def along_time(field, reim, i):
        plane = 2 * field + reim
        value = chunk(w_in, plane, i)
        value += time_term(lambda k: chunk(refs[TIME_PARTS[k][0]], 2 * TIME_PARTS[k][1] + reim, i), field)
        if field == 0:
            value -= 2.0 * TAU * chunk(z_in, reim, i)
        return value - chunk(bar, plane, i)

    def project(out, duals, radius, i):
        total = duals[0] * duals[0]
        for value in duals[1:]:
            total += value * value
        scale = jnp.minimum(1.0, radius * lax.rsqrt(total))
        for plane, value in enumerate(duals):
            out[plane, span(i), :] = value * scale

    def gradient(i, dual, out, field, vec, beta):
        duals = []
        for k in range(3):
            for reim in range(2):
                if k == 0:
                    diff = (beta * keep_time) * along_time(field, reim, i)
                else:
                    diff = (along_rows, along_cols)[k - 1](2 * field + reim, i)
                diff -= chunk(bar, 2 * (vec + k) + reim, i)
                duals.append(chunk(dual, 2 * k + reim, i) + SIGMA * diff)
        project(out, duals, ALPHA_ONE, i)

    def symmetric(i, dual, out, vec, beta):
        duals = [None] * 12
        for reim in range(2):
            p0, p1, p2 = (2 * (vec + k) + reim for k in range(3))
            steps = (
                (SIGMA * beta * keep_time) * along_time(vec, reim, i),
                SIGMA * along_rows(p1, i),
                SIGMA * along_cols(p2, i),
                0.5 * SIGMA * along_rows(p0, i) + (0.5 * SIGMA * beta * keep_time) * along_time(vec + 1, reim, i),
                0.5 * SIGMA * along_cols(p0, i) + (0.5 * SIGMA * beta * keep_time) * along_time(vec + 2, reim, i),
                0.5 * SIGMA * (along_cols(p1, i) + along_rows(p2, i)),
            )
            for k, diff in enumerate(steps):
                duals[2 * k + reim] = chunk(dual, 2 * k + reim, i) + diff
        project(out, duals, ALPHA_ZERO, i)

    def second(i):
        gradient(i, g1, g1_out, 0, 2, BETA_ONE)
        gradient(i, g2, g2_out, 1, 5, BETA_TWO)
        symmetric(i, s1, s1_out, 2, BETA_ONE)
        symmetric(i, s2, s2_out, 5, BETA_TWO)

    for part in range(4):
        rows = pl.ds(16 * part, 16)
        second(2 * part)
        second(2 * part + 1)
        for k, (source, target) in enumerate(((g1_out, g1_hbm), (g2_out, g2_hbm), (s1_out, s1_hbm), (s2_out, s2_hbm))):
            copy = pltpu.make_async_copy(source.at[:, rows, :], target.at[:, rows, :], sems.at[4 + 4 * part + k])
            copy.start()
            copies.append(copy)
    for copy in copies:
        copy.wait()


def shape(*dims):
    return jax.ShapeDtypeStruct(dims, F32)


def call(kernel, outs, ins, cost, in_specs=None, scratch=(), out_space=pltpu.VMEM):
    return pl.pallas_call(
        kernel,
        out_shape=outs,
        in_specs=in_specs or [pl.BlockSpec(memory_space=pltpu.VMEM)] * len(ins),
        out_specs=[pl.BlockSpec(memory_space=out_space)] * len(outs),
        scratch_shapes=list(scratch),
        compiler_params=pltpu.CompilerParams(vmem_limit_bytes=LIMIT),
        cost_estimate=pl.CostEstimate(flops=500 * cost, bytes_accessed=cost, transcendentals=0),
    )(*ins)


def turn(block, distance):
    return lax.ppermute(block, "row", [(i, (i + distance) % ROWS) for i in range(ROWS)])


def body(
    image_now, split_now, vector_one, vector_two, kspace_dual, grad_one, grad_two, sym_one, sym_two,
    measured, sensitivity, sampled,
):
    planes = lambda x: x.reshape(-1, BLOCK, LENGTH)
    img, spl, v1, v2, kd = map(planes, (image_now, split_now, vector_one, vector_two, kspace_dual))
    g1, g2, s1, s2, meas, sens = map(planes, (grad_one, grad_two, sym_one, sym_two, measured, sensitivity))
    first_high, first_low, high, low = map(jnp.asarray, dft_tables())
    frames = lax.axis_size("tm")
    groups = lax.axis_size("coil")
    blocks = (shape(BLOCK, 384), shape(BLOCK + 16, 384), shape(BLOCK, 384), shape(BLOCK, 384))
    hbm = pl.BlockSpec(memory_space=pltpu.HBM)
    a0, a1, a2, a3 = call(
        start_kernel, blocks,
        [pltpu.with_memory_space_constraint(x, pltpu.HBM) for x in (kd, sampled, first_high, first_low, g1, g2, s1, s2)],
        1,
        in_specs=[hbm] * 8,
        scratch=[
            pltpu.VMEM((2 * COIL, BLOCK, LENGTH), F32), pltpu.VMEM((1, LENGTH), jnp.int32),
            pltpu.VMEM((LENGTH, 2 * LENGTH), BF16), pltpu.VMEM((LENGTH, 2 * LENGTH), BF16),
            pltpu.VMEM((16, 8, LENGTH), F32), pltpu.SemaphoreType.DMA((12,)),
        ],
    )
    b2, b1, b3 = turn(a2, 2), turn(a1, 1), turn(a3, 3)
    after = [(i, i + 1) for i in range(frames - 1)]
    q_first, q_out = call(
        pack_kernel, (shape(2 * BLOCK + 16, LENGTH), shape(14, BLOCK, LENGTH)), (g1, g2, s1, s2, a0), 100_000_000,
        in_specs=[pl.BlockSpec(memory_space=pltpu.VMEM)] * 4 + [pl.BlockSpec(memory_space=pl.ANY)],
    )
    q_first = lax.ppermute(q_first, "tm", after)
    (partial,) = call(combine_kernel, (shape(2, BLOCK, LENGTH),), (a0, b1, b2, b3, high, low, sens), 200_000_000)
    partner = ((1, 0, 3, 2), (3, 2, 1, 0))
    swaps = [
        [(t * groups + c, t * groups + partner[(t + turn) % 2][c]) for t in range(frames) for c in range(groups)]
        for turn in range(2)
    ]
    w_out, w_top = call(
        plain_kernel, (shape(16, BLOCK, LENGTH), shape(16, LENGTH)),
        (img, spl, v1, v2, g1, g2, s1, s2, b1, partial), 100_000_000,
        in_specs=[pl.BlockSpec(memory_space=pltpu.VMEM)] * 9 + [pl.BlockSpec(memory_space=pl.ANY)],
    )
    pairs = []
    for t in range(1, frames):
        for c in range(groups):
            to = c if t % 2 else ((c + 1) % groups if t % 4 == 2 else (c - 1) % groups)
            pairs.append((t * groups + c, (t - 1) * groups + to))
    received = lax.ppermute(partial, ("tm", "coil"), swaps[0])
    partial, received, w_out = lax.optimization_barrier((partial, received, w_out))
    pair = partial + received
    rest = lax.ppermute(pair, ("tm", "coil"), swaps[1])
    q_in = lax.ppermute(q_out, "tm", after)
    w_in = lax.ppermute(w_out, ("tm", "coil"), pairs)
    c_blocks = (shape(BLOCK, 384), shape(BLOCK, 384), shape(BLOCK, 384), shape(BLOCK + 16, 384))
    c0, c1, c2, c3, z, q0 = call(
        predict_kernel, (*c_blocks, shape(2, BLOCK, LENGTH), shape(2, BLOCK, LENGTH)),
        (pair, rest, w_out, w_top, q_first, first_high, first_low, sens), 200_000_000,
    )
    n2, n1, n3 = turn(c2, 2), turn(c1, 1), turn(c3, 3)
    z_in = lax.ppermute(z, "tm", [(i + 1, i) for i in range(frames - 1)])
    like = lambda x: shape(*x.shape)
    fields = call(
        fields_kernel, tuple(map(like, (img, spl, v1, v2, g1, g2, s1, s2))),
        (img, spl, v1, v2, g1, g2, s1, s2, w_out, q0, q_in, w_in, z, z_in, n3), 1,
        scratch=[
            pltpu.VMEM((16, BLOCK + 8, LENGTH), F32),
            *(pltpu.VMEM(x.shape, F32) for x in (img, spl, v1, v2, g1, g2, s1, s2)),
            pltpu.SemaphoreType.DMA((20,)),
        ],
        out_space=pltpu.HBM,
    )
    vmem = pl.BlockSpec(memory_space=pltpu.VMEM)
    (kspace,) = call(
        finish_kernel, (like(kd),),
        (c0, n1, n2, n3, high, low, kd, meas, pltpu.with_memory_space_constraint(sampled, pltpu.HBM)), 4_000_000,
        in_specs=[vmem] * 8 + [hbm],
        scratch=[
            pltpu.VMEM((1, LENGTH), jnp.int32), pltpu.VMEM(kd.shape, F32), pltpu.SemaphoreType.DMA((1 + 2 * COIL,)),
        ],
        out_space=pltpu.HBM,
    )
    img_new, spl_new, v1_new, v2_new, g1_new, g2_new, s1_new, s2_new = fields
    news = (img_new, spl_new, v1_new, v2_new, kspace, g1_new, g2_new, s1_new, s2_new)
    olds = (image_now, split_now, vector_one, vector_two, kspace_dual, grad_one, grad_two, sym_one, sym_two)
    return tuple(new.reshape(old.shape) for new, old in zip(news, olds))


def solution(mesh):
    image = P(None, "tm", "row", None)
    vector = P(None, None, "tm", "row", None)
    kspace = P(None, "tm", "coil", "row", None)
    return jax.shard_map(
        body,
        mesh=mesh,
        in_specs=(
            image, image, vector, vector, kspace, vector, vector, vector, vector, kspace,
            P(None, "coil", "row", None), P("tm", None),
        ),
        out_specs=(image, image, vector, vector, kspace, vector, vector, vector, vector),
        check_vma=False,
    )
```

```python
import functools
import math

import jax
import jax.numpy as jnp
import ml_dtypes
import numpy as np
from jax import lax
from jax.experimental import pallas as pl
from jax.experimental.pallas import tpu as pltpu
from jax.sharding import PartitionSpec as P

TAU = 0.25
SIGMA = 0.25
LAMBDA_DATA = 2.0
ALPHA_ONE = 2.0
ALPHA_ZERO = 1.2
BETA_ONE = 2.0
BETA_TWO = 0.5

LENGTH = 256
COIL = 3
BLOCK = 64
ROWS = 4
F32 = jnp.float32
BF16 = jnp.bfloat16
LIMIT = 12 * 1024 * 1024


def halves(table):
    high = table.astype(ml_dtypes.bfloat16)
    return high, (table - high.astype(np.float64)).astype(ml_dtypes.bfloat16)


def dft_tables():
    positions = np.arange(LENGTH)
    angles = (positions[:, None] * positions[None, :] % LENGTH) * (2.0 * math.pi / LENGTH)
    real = np.cos(angles) / math.sqrt(LENGTH)
    imag = np.sin(angles) / math.sqrt(LENGTH)
    of_real = np.concatenate([real, imag], axis=1).reshape(ROWS, 1, BLOCK, 2 * LENGTH)
    of_imag = np.concatenate([-imag, real], axis=1).reshape(ROWS, 1, BLOCK, 2 * LENGTH)
    table = np.concatenate([of_real, of_imag], axis=1).reshape(2 * LENGTH, 2 * LENGTH)
    return halves(of_real.reshape(LENGTH, 2 * LENGTH)) + halves(table)


def split(values):
    high = values.astype(BF16)
    return high, (values - high.astype(F32)).astype(BF16)


def dot_nt(a, b):
    return lax.dot_general(a, b, (((1,), (1,)), ((), ())), preferred_element_type=F32)


def dot_nn(a, b):
    return lax.dot_general(a, b, (((1,), (0,)), ((), ())), preferred_element_type=F32)


def first_transform(table_high, table_low, right, row):
    def blocks(ref):
        return jnp.concatenate(
            [ref[pl.ds(pl.multiple_of(lax.rem(row + d, ROWS) * BLOCK, BLOCK), BLOCK), :] for d in range(ROWS)], axis=0
        )

    high, low = split(right)
    left_high = blocks(table_high)
    return dot_nt(left_high, high) + (dot_nt(left_high, low) + dot_nt(blocks(table_low), high))


def second_transform(table_high, table_low, received, row):
    def blocks(ref):
        return jnp.concatenate(
            [ref[pl.ds(pl.multiple_of(lax.rem(row + ROWS - d, ROWS) * 128, 128), 128), :] for d in range(ROWS)], axis=0
        )

    left = jnp.concatenate(
        [
            jnp.concatenate([block[:BLOCK, 128 * c : 128 * (c + 1)] for block in received], axis=1)
            for c in range(COIL)
        ],
        axis=0,
    )
    high, low = split(left)
    right_high = blocks(table_high)
    return dot_nn(high, right_high) + (dot_nn(low, right_high) + dot_nn(high, blocks(table_low)))


def iota(shape, dimension):
    return lax.broadcasted_iota(jnp.int32, shape, dimension)


ROW_PARTS = (("g1", 1), ("g2", 1), ("s1", 1), ("s1", 3), ("s1", 5), ("s2", 1), ("s2", 3), ("s2", 5))
TIME_PARTS = (("g1", 0), ("g2", 0), ("s1", 0), ("s1", 3), ("s1", 4), ("s2", 0), ("s2", 3), ("s2", 4))


def start_kernel(
    kd_hbm, lines_hbm, th_hbm, tl_hbm, g1, g2, s1, s2, o0, o1, o2, o3, mask_out,
    kd_ref, lines_ref, th_ref, tl_ref, ends, sems
):
    row = lax.axis_index("row")
    copies = [
        pltpu.make_async_copy(source, target, sems.at[k])
        for k, (source, target) in enumerate(
            ((kd_hbm, kd_ref), (lines_hbm, lines_ref), (th_hbm, th_ref), (tl_hbm, tl_ref))
        )
    ]
    refs = dict(g1=g1, g2=g2, s1=s1, s2=s2)
    for index, (name, part) in enumerate(ROW_PARTS):
        copies.append(
            pltpu.make_async_copy(
                refs[name].at[2 * part : 2 * part + 2, BLOCK - 8 : BLOCK, :],
                ends.at[2 * index : 2 * index + 2],
                sems.at[4 + index],
            )
        )
    for copy in copies:
        copy.start()
    for copy in copies[:4]:
        copy.wait()
    mask = lines_ref[...].astype(F32)
    mask_out[...] = mask
    parts = []
    for c in range(COIL):
        real = kd_ref[c] * mask
        imag = kd_ref[COIL + c] * mask
        parts.append(jnp.concatenate([real, -imag], axis=1))
        parts.append(jnp.concatenate([imag, real], axis=1))
    out = first_transform(th_ref, tl_ref, jnp.concatenate(parts, axis=0), row)
    for d, ref in enumerate((o0, o1, o2, o3)):
        ref[0:BLOCK, :] = out[BLOCK * d : BLOCK * (d + 1)]
    for copy in copies[4:]:
        copy.wait()
    o1[BLOCK:, LENGTH:] = jnp.zeros((16, 128), F32)
    for plane in range(16):
        o1[BLOCK + plane : BLOCK + plane + 1, 0:LENGTH] = ends[plane, 7:8, :]


def chunk(ref, plane, i):
    return ref[plane, pl.ds(i * 8 if isinstance(i, int) else pl.multiple_of(i * 8, 8), 8), :]


def pack_kernel(g1, g2, s1, s2, order, q_first):
    refs = dict(g1=g1, g2=g2, s1=s1, s2=s2)
    for reim in range(2):
        q_first[BLOCK * reim : BLOCK * (reim + 1), :] = g1[reim]
        tops = [refs[name][2 * part + reim, 0:1, :] for name, part in TIME_PARTS]
        for field in range(8):
            place = 2 * BLOCK + 2 * field + reim
            q_first[place : place + 1, :] = time_term(lambda k: tops[k], field)


def plain_kernel(img, spl, v1, v2, g1, g2, s1, s2, b1, q_first, order, w_out, image_out, tops, to_core, to_chip):
    odd = lax.rem(lax.axis_index("tm"), 2)
    row = lax.axis_index("row")
    keep_time = (lax.axis_index("tm") != lax.axis_size("tm") - 1).astype(F32)
    refs = dict(g1=g1, g2=g2, s1=s1, s2=s2)
    edge = jnp.where(row == 0, 0.0, b1[BLOCK:, 0:LENGTH])
    where = {part: 2 * index for index, part in enumerate(ROW_PARTS)}

    def step(i, carry):
        rows = iota((8, LENGTH), 0)
        cols = iota((8, LENGTH), 1)
        drop_row = (rows == 7) & (i == 7) & (row == ROWS - 1)

        def adj_rows(name, plane):
            ref = refs[name]
            here = chunk(ref, plane, i)
            above = chunk(ref, plane, jnp.maximum(i - 1, 0))
            at = where[name, plane // 2] + plane % 2
            above = jnp.where(i == 0, edge[at : at + 1], above)
            behind = jnp.where(rows == 0, pltpu.roll(above, 1, 0), pltpu.roll(here, 1, 0))
            return behind - jnp.where(drop_row, 0.0, here)

        def adj_cols(ref, plane):
            here = chunk(ref, plane, i)
            behind = jnp.where(cols == 0, 0.0, pltpu.roll(here, 1, 1))
            return behind - jnp.where(cols == LENGTH - 1, 0.0, here)

        def put(ref, plane, value):
            ref[plane, pl.ds(pl.multiple_of(i * 8, 8), 8), :] = value

        for reim in range(2):
            z, y, x = reim, 2 + reim, 4 + reim
            one = -BETA_ONE * keep_time * chunk(g1, z, i) + adj_rows("g1", y) + adj_cols(g1, x)
            two = -BETA_TWO * keep_time * chunk(g2, z, i) + adj_rows("g2", y) + adj_cols(g2, x)
            image = chunk(img, reim, i) - 2.0 * TAU * one
            other = chunk(spl, reim, i) - 2.0 * TAU * (two - one)
            before = q_first[pl.ds(pl.multiple_of(BLOCK * reim + i * 8, 8), 8), :]
            put(image_out, reim, image - 2.0 * TAU * BETA_ONE * before)
            put(w_out, reim, image - other)
            put(w_out, 2 + reim, other)
            for base, vec, grad, name, beta in ((4, v1, g1, "s1", BETA_ONE), (10, v2, g2, "s2", BETA_TWO)):
                sym = refs[name]
                p0, p1, p2, p3, p4, p5 = (2 * k + reim for k in range(6))
                first = -beta * keep_time * chunk(sym, p0, i) + 0.5 * (adj_rows(name, p3) + adj_cols(sym, p4))
                second = adj_rows(name, p1) - 0.5 * beta * keep_time * chunk(sym, p3, i) + 0.5 * adj_cols(sym, p5)
                third = adj_cols(sym, p2) - 0.5 * beta * keep_time * chunk(sym, p4, i) + 0.5 * adj_rows(name, p5)
                for k, adjoint in enumerate((first, second, third)):
                    value = chunk(vec, 2 * k + reim, i) - 2.0 * TAU * (adjoint - chunk(grad, 2 * k + reim, i))
                    put(w_out, base + 2 * k + reim, value)
        return carry

    lax.fori_loop(0, 8, step, 0)
    for plane in range(16):
        place = 2 * BLOCK + plane
        tops[plane : plane + 1, :] = w_out[plane, 0:1, :] + q_first[place : place + 1, :]

    def messages(q_to, w_to):
        for index, (name, part) in enumerate(TIME_PARTS):
            q_to[2 * index : 2 * index + 2] = refs[name][2 * part : 2 * part + 2]
        w_to[...] = w_out[...]

    pl.when(odd == 0)(lambda: messages(to_core, to_chip))
    pl.when(odd == 1)(lambda: messages(to_chip, to_core))


def combine_kernel(b0, b1, b2, b3, th_ref, tl_ref, sens, out):
    row = lax.axis_index("row")
    both = second_transform(th_ref, tl_ref, (b0, b1, b2, b3), row)
    real_sum = None
    for c in range(COIL):
        real = both[BLOCK * c : BLOCK * (c + 1), :LENGTH]
        imag = both[BLOCK * c : BLOCK * (c + 1), LENGTH:]
        real_term = sens[c] * real + sens[COIL + c] * imag
        imag_term = sens[c] * imag - sens[COIL + c] * real
        real_sum = real_term if real_sum is None else real_sum + real_term
        imag_sum = imag_term if c == 0 else imag_sum + imag_term
    out[0] = real_sum
    out[1] = imag_sum


def time_term(q, field):
    if field == 0:
        return -2.0 * TAU * (2.0 * BETA_ONE * q(0) - BETA_TWO * q(1))
    if field == 1:
        return -2.0 * TAU * (BETA_TWO * q(1) - BETA_ONE * q(0))
    beta = BETA_ONE if field < 5 else BETA_TWO
    return (-2.0 * TAU * beta * (1.0 if field in (2, 5) else 0.5)) * q(field)


def predict_kernel(sum_a, sum_b, base, tops, th_ref, tl_ref, sens, o0, o1, o2, o3, z_out):
    row = lax.axis_index("row")
    image = []
    for reim in range(2):
        back = sum_a[reim] + sum_b[reim]
        z_out[reim] = back
        image.append(base[reim] - 2.0 * TAU * back)
    parts = []
    for c in range(COIL):
        real = sens[c] * image[0] - sens[COIL + c] * image[1]
        imag = sens[c] * image[1] + sens[COIL + c] * image[0]
        parts.append(jnp.concatenate([real, imag], axis=1))
        parts.append(jnp.concatenate([-imag, real], axis=1))
    out = first_transform(th_ref, tl_ref, jnp.concatenate(parts, axis=0), row)
    for d, ref in enumerate((o0, o1, o2, o3)):
        ref[0:BLOCK, :] = out[BLOCK * d : BLOCK * (d + 1)]
    o3[BLOCK:, LENGTH:] = jnp.zeros((16, 128), F32)
    o3[BLOCK:, 0:LENGTH] = tops[...]
    for reim in range(2):
        o3[BLOCK + reim : BLOCK + reim + 1, 0:LENGTH] -= 2.0 * TAU * (sum_a[reim, 0:1, :] + sum_b[reim, 0:1, :])


def finish_kernel(b0, b1, b2, b3, th_ref, tl_ref, kd_ref, measured, mask_ref, out_hbm, out, sems):
    row = lax.axis_index("row")
    both = second_transform(th_ref, tl_ref, (b0, b1, b2, b3), row)
    mask = SIGMA * mask_ref[...]
    scale = 1.0 / (1.0 + SIGMA / LAMBDA_DATA)
    copies = []
    for c in range(COIL):
        real = both[BLOCK * c : BLOCK * (c + 1), :LENGTH]
        imag = -both[BLOCK * c : BLOCK * (c + 1), LENGTH:]
        for plane, value in ((c, real), (COIL + c, imag)):
            out[plane] = (kd_ref[plane] + mask * (value - measured[plane])) * scale
            copies.append(pltpu.make_async_copy(out.at[plane], out_hbm.at[plane], sems.at[plane]))
            copies[-1].start()
    for copy in copies:
        copy.wait()


def fields_kernel(
    img, spl, v1, v2, g1, g2, s1, s2, w, from_core, from_chip, z, z_in, n3,
    img_hbm, spl_hbm, v1_hbm, v2_hbm, g1_hbm, g2_hbm, s1_hbm, s2_hbm,
    bar, img_out, spl_out, v1_out, v2_out, g1_out, g2_out, s1_out, s2_out, sems,
):
    def run(q_in, w_in):
        row = lax.axis_index("row")
        keep_time = (lax.axis_index("tm") != lax.axis_size("tm") - 1).astype(F32)
        refs = dict(g1=g1, g2=g2, s1=s1, s2=s2)
        copies = [
            pltpu.make_async_copy(source, target, sems.at[k])
            for k, (source, target) in enumerate(
                ((img_out, img_hbm), (spl_out, spl_hbm), (v1_out, v1_hbm), (v2_out, v2_hbm))
            )
        ]

        def span(i):
            return pl.ds(i * 8 if isinstance(i, int) else pl.multiple_of(i * 8, 8), 8)

        def first(i, carry):
            for reim in range(2):

                def before(k):
                    return chunk(q_in, 2 * k + reim, i)

                values = []
                for field in range(8):
                    plane = 2 * field + reim
                    value = chunk(w, plane, i) + time_term(before, field)
                    if field == 0:
                        value -= 2.0 * TAU * chunk(z, reim, i)
                    bar[plane, span(i), :] = value
                    values.append(value)
                img_out[reim, span(i), :] = 0.5 * (values[0] + values[1] + chunk(img, reim, i))
                spl_out[reim, span(i), :] = 0.5 * (values[1] + chunk(spl, reim, i))
                for k in range(3):
                    plane = 2 * k + reim
                    v1_out[plane, span(i), :] = 0.5 * (values[2 + k] + chunk(v1, plane, i))
                    v2_out[plane, span(i), :] = 0.5 * (values[5 + k] + chunk(v2, plane, i))
            return carry

        lax.fori_loop(0, 8, first, 0, unroll=2)
        for copy in copies:
            copy.start()
        for plane in range(16):
            below = n3[BLOCK + plane : BLOCK + plane + 1, 0:LENGTH]
            bar[plane, BLOCK : BLOCK + 1, :] = jnp.where(row == ROWS - 1, bar[plane, BLOCK - 1 : BLOCK, :], below)

        def along_rows(plane, i):
            here = chunk(bar, plane, i)
            below = chunk(bar, plane, i + 1)
            rows = iota((8, LENGTH), 0)
            return jnp.where(rows == 7, pltpu.roll(below, 7, 0), pltpu.roll(here, 7, 0)) - here

        def along_cols(plane, i):
            here = chunk(bar, plane, i)
            cols = iota((8, LENGTH), 1)
            return jnp.where(cols == LENGTH - 1, 0.0, pltpu.roll(here, LENGTH - 1, 1) - here)

        def along_time(field, reim, i):
            plane = 2 * field + reim
            value = chunk(w_in, plane, i)
            value += time_term(lambda k: chunk(refs[TIME_PARTS[k][0]], 2 * TIME_PARTS[k][1] + reim, i), field)
            if field == 0:
                value -= 2.0 * TAU * chunk(z_in, reim, i)
            return value - chunk(bar, plane, i)

        def project(out, duals, radius, i):
            total = duals[0] * duals[0]
            for value in duals[1:]:
                total += value * value
            scale = jnp.minimum(1.0, radius * lax.rsqrt(total))
            for plane, value in enumerate(duals):
                out[plane, span(i), :] = value * scale

        def gradient(i, dual, out, field, vec, beta):
            duals = []
            for k in range(3):
                for reim in range(2):
                    if k == 0:
                        diff = (beta * keep_time) * along_time(field, reim, i)
                    else:
                        diff = (along_rows, along_cols)[k - 1](2 * field + reim, i)
                    diff -= chunk(bar, 2 * (vec + k) + reim, i)
                    duals.append(chunk(dual, 2 * k + reim, i) + SIGMA * diff)
            project(out, duals, ALPHA_ONE, i)

        def symmetric(i, dual, out, vec, beta):
            duals = [None] * 12
            for reim in range(2):
                p0, p1, p2 = (2 * (vec + k) + reim for k in range(3))
                steps = (
                    (SIGMA * beta * keep_time) * along_time(vec, reim, i),
                    SIGMA * along_rows(p1, i),
                    SIGMA * along_cols(p2, i),
                    0.5 * SIGMA * along_rows(p0, i) + (0.5 * SIGMA * beta * keep_time) * along_time(vec + 1, reim, i),
                    0.5 * SIGMA * along_cols(p0, i) + (0.5 * SIGMA * beta * keep_time) * along_time(vec + 2, reim, i),
                    0.5 * SIGMA * (along_cols(p1, i) + along_rows(p2, i)),
                )
                for k, diff in enumerate(steps):
                    duals[2 * k + reim] = chunk(dual, 2 * k + reim, i) + diff
            project(out, duals, ALPHA_ZERO, i)

        def second(i):
            gradient(i, g1, g1_out, 0, 2, BETA_ONE)
            gradient(i, g2, g2_out, 1, 5, BETA_TWO)
            symmetric(i, s1, s1_out, 2, BETA_ONE)
            symmetric(i, s2, s2_out, 5, BETA_TWO)

        for part in range(4):
            rows = pl.ds(16 * part, 16)
            second(2 * part)
            second(2 * part + 1)
            for k, (source, target) in enumerate(((g1_out, g1_hbm), (g2_out, g2_hbm), (s1_out, s1_hbm), (s2_out, s2_hbm))):
                copy = pltpu.make_async_copy(source.at[:, rows, :], target.at[:, rows, :], sems.at[4 + 4 * part + k])
                copy.start()
                copies.append(copy)
        for copy in copies:
            copy.wait()

    odd = lax.rem(lax.axis_index("tm"), 2)
    pl.when(odd == 0)(lambda: run(from_chip, from_core))
    pl.when(odd == 1)(lambda: run(from_core, from_chip))


def shape(*dims):
    return jax.ShapeDtypeStruct(dims, F32)


def call(kernel, outs, ins, cost, in_specs=None, scratch=(), out_space=pltpu.VMEM):
    return pl.pallas_call(
        kernel,
        out_shape=outs,
        in_specs=in_specs or [pl.BlockSpec(memory_space=pltpu.VMEM)] * len(ins),
        out_specs=[pl.BlockSpec(memory_space=out_space)] * len(outs),
        scratch_shapes=list(scratch),
        compiler_params=pltpu.CompilerParams(vmem_limit_bytes=LIMIT),
        cost_estimate=pl.CostEstimate(flops=500 * cost, bytes_accessed=cost, transcendentals=0),
    )(*ins)


def turn(block, distance):
    return lax.ppermute(block, "row", [(i, (i + distance) % ROWS) for i in range(ROWS)])


def body(
    image_now, split_now, vector_one, vector_two, kspace_dual, grad_one, grad_two, sym_one, sym_two,
    measured, sensitivity, sampled,
):
    planes = lambda x: x.reshape(-1, BLOCK, LENGTH)
    img, spl, v1, v2, kd = map(planes, (image_now, split_now, vector_one, vector_two, kspace_dual))
    g1, g2, s1, s2, meas, sens = map(planes, (grad_one, grad_two, sym_one, sym_two, measured, sensitivity))
    first_high, first_low, high, low = map(jnp.asarray, dft_tables())
    frames = lax.axis_size("tm")
    groups = lax.axis_size("coil")
    blocks = (shape(BLOCK, 384), shape(BLOCK + 16, 384), shape(BLOCK, 384), shape(BLOCK, 384))
    hbm = pl.BlockSpec(memory_space=pltpu.HBM)
    a0, a1, a2, a3, mask = call(
        start_kernel, (*blocks, shape(1, LENGTH)),
        [pltpu.with_memory_space_constraint(x, pltpu.HBM) for x in (kd, sampled, first_high, first_low, g1, g2, s1, s2)],
        1,
        in_specs=[hbm] * 8,
        scratch=[
            pltpu.VMEM((2 * COIL, BLOCK, LENGTH), F32), pltpu.VMEM((1, LENGTH), jnp.int32),
            pltpu.VMEM((LENGTH, 2 * LENGTH), BF16), pltpu.VMEM((LENGTH, 2 * LENGTH), BF16),
            pltpu.VMEM((16, 8, LENGTH), F32), pltpu.SemaphoreType.DMA((12,)),
        ],
    )
    b2, b1, b3 = turn(a2, 2), turn(a1, 1), turn(a3, 3)
    after = [(i, i + 1) for i in range(frames - 1)]
    (q_first,) = call(
        pack_kernel, (shape(2 * BLOCK + 16, LENGTH),), (g1, g2, s1, s2, a0), 100_000_000,
        in_specs=[pl.BlockSpec(memory_space=pltpu.VMEM)] * 4 + [pl.BlockSpec(memory_space=pl.ANY)],
    )
    q_first = lax.ppermute(q_first, "tm", after)
    (partial,) = call(combine_kernel, (shape(2, BLOCK, LENGTH),), (a0, b1, b2, b3, high, low, sens), 200_000_000)
    partner = ((1, 0, 3, 2), (3, 2, 1, 0))
    swaps = [
        [(t * groups + c, t * groups + partner[(t + turn) % 2][c]) for t in range(frames) for c in range(groups)]
        for turn in range(2)
    ]
    stack = shape(16, BLOCK, LENGTH)
    w_out, base, tops, to_core, to_chip = call(
        plain_kernel, (stack, shape(2, BLOCK, LENGTH), shape(16, LENGTH), stack, stack),
        (img, spl, v1, v2, g1, g2, s1, s2, b1, q_first, partial), 100_000_000,
        in_specs=[pl.BlockSpec(memory_space=pltpu.VMEM)] * 10 + [pl.BlockSpec(memory_space=pl.ANY)],
    )
    received = lax.ppermute(partial, ("tm", "coil"), swaps[0])
    partial, received, w_out = lax.optimization_barrier((partial, received, w_out))
    pair = partial + received
    rest = lax.ppermute(pair, ("tm", "coil"), swaps[1])
    pairs = []
    for t in range(1, frames - 1, 2):
        for c in range(groups):
            there = c if t % 4 == 1 else (c + 1) % groups
            pairs.append((t * groups + c, (t + 1) * groups + there))
            pairs.append(((t + 1) * groups + there, t * groups + c))
    from_chip = lax.ppermute(to_chip, ("tm", "coil"), pairs)
    from_core = lax.ppermute(to_core, "tm", [(t, t ^ 1) for t in range(frames)])
    c_blocks = (shape(BLOCK, 384), shape(BLOCK, 384), shape(BLOCK, 384), shape(BLOCK + 16, 384))
    c0, c1, c2, c3, z = call(
        predict_kernel, (*c_blocks, shape(2, BLOCK, LENGTH)),
        (pair, rest, base, tops, first_high, first_low, sens), 200_000_000,
    )
    n2, n1, n3 = turn(c2, 2), turn(c1, 1), turn(c3, 3)
    z, from_core = lax.optimization_barrier((z, from_core))
    z_in = lax.ppermute(z, "tm", [(i + 1, i) for i in range(frames - 1)])
    like = lambda x: shape(*x.shape)
    fields = call(
        fields_kernel, tuple(map(like, (img, spl, v1, v2, g1, g2, s1, s2))),
        (img, spl, v1, v2, g1, g2, s1, s2, w_out, from_core, from_chip, z, z_in, n3), 1,
        scratch=[
            pltpu.VMEM((16, BLOCK + 8, LENGTH), F32),
            *(pltpu.VMEM(x.shape, F32) for x in (img, spl, v1, v2, g1, g2, s1, s2)),
            pltpu.SemaphoreType.DMA((20,)),
        ],
        out_space=pltpu.HBM,
    )
    (kspace,) = call(
        finish_kernel, (like(kd),), (c0, n1, n2, n3, high, low, kd, meas, mask), 4_000_000,
        scratch=[pltpu.VMEM(kd.shape, F32), pltpu.SemaphoreType.DMA((2 * COIL,))],
        out_space=pltpu.HBM,
    )
    img_new, spl_new, v1_new, v2_new, g1_new, g2_new, s1_new, s2_new = fields
    news = (img_new, spl_new, v1_new, v2_new, kspace, g1_new, g2_new, s1_new, s2_new)
    olds = (image_now, split_now, vector_one, vector_two, kspace_dual, grad_one, grad_two, sym_one, sym_two)
    return tuple(new.reshape(old.shape) for new, old in zip(news, olds))


def solution(mesh):
    image = P(None, "tm", "row", None)
    vector = P(None, None, "tm", "row", None)
    kspace = P(None, "tm", "coil", "row", None)
    return jax.shard_map(
        body,
        mesh=mesh,
        in_specs=(
            image, image, vector, vector, kspace, vector, vector, vector, vector, kspace,
            P(None, "coil", "row", None), P("tm", None),
        ),
        out_specs=(image, image, vector, vector, kspace, vector, vector, vector, vector),
        check_vma=False,
    )
```

```python
import functools
import math

import jax
import jax.numpy as jnp
import ml_dtypes
import numpy as np
from jax import lax
from jax.experimental import pallas as pl
from jax.experimental.pallas import tpu as pltpu
from jax.sharding import PartitionSpec as P

TAU = 0.25
SIGMA = 0.25
LAMBDA_DATA = 2.0
ALPHA_ONE = 2.0
ALPHA_ZERO = 1.2
BETA_ONE = 2.0
BETA_TWO = 0.5

LENGTH = 256
COIL = 3
BLOCK = 64
ROWS = 4
F32 = jnp.float32
BF16 = jnp.bfloat16
LIMIT = 12 * 1024 * 1024


def halves(table):
    high = table.astype(ml_dtypes.bfloat16)
    return high, (table - high.astype(np.float64)).astype(ml_dtypes.bfloat16)


def dft_tables():
    positions = np.arange(LENGTH)
    angles = (positions[:, None] * positions[None, :] % LENGTH) * (2.0 * math.pi / LENGTH)
    real = np.cos(angles) / math.sqrt(LENGTH)
    imag = np.sin(angles) / math.sqrt(LENGTH)
    of_real = np.concatenate([real, imag], axis=1).reshape(ROWS, 1, BLOCK, 2 * LENGTH)
    of_imag = np.concatenate([-imag, real], axis=1).reshape(ROWS, 1, BLOCK, 2 * LENGTH)
    table = np.concatenate([of_real, of_imag], axis=1).reshape(2 * LENGTH, 2 * LENGTH)
    return halves(of_real.reshape(LENGTH, 2 * LENGTH)) + halves(table)


def split(values):
    high = values.astype(BF16)
    return high, (values - high.astype(F32)).astype(BF16)


def dot_nt(a, b):
    return lax.dot_general(a, b, (((1,), (1,)), ((), ())), preferred_element_type=F32)


def dot_nn(a, b):
    return lax.dot_general(a, b, (((1,), (0,)), ((), ())), preferred_element_type=F32)


def first_transform(table_high, table_low, right, row):
    def blocks(ref):
        return jnp.concatenate(
            [ref[pl.ds(pl.multiple_of(lax.rem(row + d, ROWS) * BLOCK, BLOCK), BLOCK), :] for d in range(ROWS)], axis=0
        )

    high, low = split(right)
    left_high = blocks(table_high)
    return dot_nt(left_high, high) + (dot_nt(left_high, low) + dot_nt(blocks(table_low), high))


def second_transform(table_high, table_low, received, row):
    def blocks(ref):
        return jnp.concatenate(
            [ref[pl.ds(pl.multiple_of(lax.rem(row + ROWS - d, ROWS) * 128, 128), 128), :] for d in range(ROWS)], axis=0
        )

    left = jnp.concatenate(
        [
            jnp.concatenate([block[:BLOCK, 128 * c : 128 * (c + 1)] for block in received], axis=1)
            for c in range(COIL)
        ],
        axis=0,
    )
    high, low = split(left)
    right_high = blocks(table_high)
    return dot_nn(high, right_high) + (dot_nn(low, right_high) + dot_nn(high, blocks(table_low)))


def iota(shape, dimension):
    return lax.broadcasted_iota(jnp.int32, shape, dimension)


ROW_PARTS = (("g1", 1), ("g2", 1), ("s1", 1), ("s1", 3), ("s1", 5), ("s2", 1), ("s2", 3), ("s2", 5))
TIME_PARTS = (("g1", 0), ("g2", 0), ("s1", 0), ("s1", 3), ("s1", 4), ("s2", 0), ("s2", 3), ("s2", 4))


def start_kernel(
    kd_hbm, lines_hbm, th_hbm, tl_hbm, g1, g2, s1, s2, o0, o1, o2, o3, mask_out,
    kd_ref, lines_ref, th_ref, tl_ref, ends, sems
):
    row = lax.axis_index("row")
    copies = [
        pltpu.make_async_copy(source, target, sems.at[k])
        for k, (source, target) in enumerate(
            ((kd_hbm, kd_ref), (lines_hbm, lines_ref), (th_hbm, th_ref), (tl_hbm, tl_ref))
        )
    ]
    refs = dict(g1=g1, g2=g2, s1=s1, s2=s2)
    for index, (name, part) in enumerate(ROW_PARTS):
        copies.append(
            pltpu.make_async_copy(
                refs[name].at[2 * part : 2 * part + 2, BLOCK - 8 : BLOCK, :],
                ends.at[2 * index : 2 * index + 2],
                sems.at[4 + index],
            )
        )
    for copy in copies:
        copy.start()
    for copy in copies[:4]:
        copy.wait()
    mask = lines_ref[...].astype(F32)
    mask_out[...] = mask
    parts = []
    for c in range(COIL):
        real = kd_ref[c] * mask
        imag = kd_ref[COIL + c] * mask
        parts.append(jnp.concatenate([real, -imag], axis=1))
        parts.append(jnp.concatenate([imag, real], axis=1))
    out = first_transform(th_ref, tl_ref, jnp.concatenate(parts, axis=0), row)
    for d, ref in enumerate((o0, o1, o2, o3)):
        ref[0:BLOCK, :] = out[BLOCK * d : BLOCK * (d + 1)]
    for copy in copies[4:]:
        copy.wait()
    o1[BLOCK:, LENGTH:] = jnp.zeros((16, 128), F32)
    for plane in range(16):
        o1[BLOCK + plane : BLOCK + plane + 1, 0:LENGTH] = ends[plane, 7:8, :]


def rows_at(start):
    return pl.ds(start if isinstance(start, int) else pl.multiple_of(start, 8), 8)


def chunk(ref, plane, i):
    return ref[plane, rows_at(i * 8), :]


def pack_kernel(g1, g2, s1, s2, order, q_first):
    refs = dict(g1=g1, g2=g2, s1=s1, s2=s2)
    for reim in range(2):
        q_first[BLOCK * reim : BLOCK * (reim + 1), :] = g1[reim]
        tops = [refs[name][2 * part + reim, 0:1, :] for name, part in TIME_PARTS]
        for field in range(8):
            place = 2 * BLOCK + 2 * field + reim
            q_first[place : place + 1, :] = time_term(lambda k: tops[k], field)


def plain_kernel(img, spl, v1, v2, g1, g2, s1, s2, b1, q_first, order, w_out, image_out, tops, q0_out, to_core, to_chip):
    odd = lax.rem(lax.axis_index("tm"), 2)
    row = lax.axis_index("row")
    keep_time = (lax.axis_index("tm") != lax.axis_size("tm") - 1).astype(F32)
    refs = dict(g1=g1, g2=g2, s1=s1, s2=s2)
    edge = jnp.where(row == 0, 0.0, b1[BLOCK:, 0:LENGTH])
    where = {part: 2 * index for index, part in enumerate(ROW_PARTS)}

    def step(i, carry):
        rows = iota((8, LENGTH), 0)
        cols = iota((8, LENGTH), 1)
        drop_row = (rows == 7) & (i == 7) & (row == ROWS - 1)

        def adj_rows(name, plane):
            ref = refs[name]
            here = chunk(ref, plane, i)
            above = chunk(ref, plane, jnp.maximum(i - 1, 0))
            at = where[name, plane // 2] + plane % 2
            above = jnp.where(i == 0, edge[at : at + 1], above)
            behind = jnp.where(rows == 0, pltpu.roll(above, 1, 0), pltpu.roll(here, 1, 0))
            return behind - jnp.where(drop_row, 0.0, here)

        def adj_cols(ref, plane):
            here = chunk(ref, plane, i)
            behind = jnp.where(cols == 0, 0.0, pltpu.roll(here, 1, 1))
            return behind - jnp.where(cols == LENGTH - 1, 0.0, here)

        def put(ref, plane, value):
            ref[plane, pl.ds(pl.multiple_of(i * 8, 8), 8), :] = value

        for reim in range(2):
            z, y, x = reim, 2 + reim, 4 + reim
            one = -BETA_ONE * keep_time * chunk(g1, z, i) + adj_rows("g1", y) + adj_cols(g1, x)
            two = -BETA_TWO * keep_time * chunk(g2, z, i) + adj_rows("g2", y) + adj_cols(g2, x)
            image = chunk(img, reim, i) - 2.0 * TAU * one
            other = chunk(spl, reim, i) - 2.0 * TAU * (two - one)
            before = q_first[pl.ds(pl.multiple_of(BLOCK * reim + i * 8, 8), 8), :]
            put(q0_out, reim, before)
            put(image_out, reim, image - 2.0 * TAU * BETA_ONE * before)
            put(w_out, reim, image - other)
            put(w_out, 2 + reim, other)
            for base, vec, grad, name, beta in ((4, v1, g1, "s1", BETA_ONE), (10, v2, g2, "s2", BETA_TWO)):
                sym = refs[name]
                p0, p1, p2, p3, p4, p5 = (2 * k + reim for k in range(6))
                first = -beta * keep_time * chunk(sym, p0, i) + 0.5 * (adj_rows(name, p3) + adj_cols(sym, p4))
                second = adj_rows(name, p1) - 0.5 * beta * keep_time * chunk(sym, p3, i) + 0.5 * adj_cols(sym, p5)
                third = adj_cols(sym, p2) - 0.5 * beta * keep_time * chunk(sym, p4, i) + 0.5 * adj_rows(name, p5)
                for k, adjoint in enumerate((first, second, third)):
                    value = chunk(vec, 2 * k + reim, i) - 2.0 * TAU * (adjoint - chunk(grad, 2 * k + reim, i))
                    put(w_out, base + 2 * k + reim, value)
        return carry

    lax.fori_loop(0, 8, step, 0)
    for plane in range(16):
        place = 2 * BLOCK + plane
        tops[plane : plane + 1, :] = w_out[plane, 0:1, :] + q_first[place : place + 1, :]

    def messages(q_to, w_to):
        for index, (name, part) in enumerate(TIME_PARTS[1:]):
            q_to[2 * index : 2 * index + 2] = refs[name][2 * part : 2 * part + 2]
        w_to[...] = w_out[2:]

    pl.when(odd == 0)(lambda: messages(to_core, to_chip))
    pl.when(odd == 1)(lambda: messages(to_chip, to_core))


def combine_kernel(b0, b1, b2, b3, th_ref, tl_ref, sens, out):
    row = lax.axis_index("row")
    both = second_transform(th_ref, tl_ref, (b0, b1, b2, b3), row)
    real_sum = None
    for c in range(COIL):
        real = both[BLOCK * c : BLOCK * (c + 1), :LENGTH]
        imag = both[BLOCK * c : BLOCK * (c + 1), LENGTH:]
        real_term = sens[c] * real + sens[COIL + c] * imag
        imag_term = sens[c] * imag - sens[COIL + c] * real
        real_sum = real_term if real_sum is None else real_sum + real_term
        imag_sum = imag_term if c == 0 else imag_sum + imag_term
    out[0] = real_sum
    out[1] = imag_sum


def time_term(q, field):
    if field == 0:
        return -2.0 * TAU * (2.0 * BETA_ONE * q(0) - BETA_TWO * q(1))
    if field == 1:
        return -2.0 * TAU * (BETA_TWO * q(1) - BETA_ONE * q(0))
    beta = BETA_ONE if field < 5 else BETA_TWO
    return (-2.0 * TAU * beta * (1.0 if field in (2, 5) else 0.5)) * q(field)


def predict_kernel(sum_a, sum_b, base, tops, w, th_ref, tl_ref, sens, o0, o1, o2, o3, z_out):
    row = lax.axis_index("row")
    image = []
    for reim in range(2):
        back = sum_a[reim] + sum_b[reim]
        z_out[reim] = w[reim] - 2.0 * TAU * back
        image.append(base[reim] - 2.0 * TAU * back)
    parts = []
    for c in range(COIL):
        real = sens[c] * image[0] - sens[COIL + c] * image[1]
        imag = sens[c] * image[1] + sens[COIL + c] * image[0]
        parts.append(jnp.concatenate([real, imag], axis=1))
        parts.append(jnp.concatenate([-imag, real], axis=1))
    out = first_transform(th_ref, tl_ref, jnp.concatenate(parts, axis=0), row)
    for d, ref in enumerate((o0, o1, o2, o3)):
        ref[0:BLOCK, :] = out[BLOCK * d : BLOCK * (d + 1)]
    o3[BLOCK:, LENGTH:] = jnp.zeros((16, 128), F32)
    o3[BLOCK:, 0:LENGTH] = tops[...]
    for reim in range(2):
        o3[BLOCK + reim : BLOCK + reim + 1, 0:LENGTH] -= 2.0 * TAU * (sum_a[reim, 0:1, :] + sum_b[reim, 0:1, :])


def finish_kernel(b0, b1, b2, b3, th_ref, tl_ref, kd_ref, measured, mask_ref, out_hbm, out, sems):
    row = lax.axis_index("row")
    both = second_transform(th_ref, tl_ref, (b0, b1, b2, b3), row)
    mask = SIGMA * mask_ref[...]
    scale = 1.0 / (1.0 + SIGMA / LAMBDA_DATA)
    copies = []
    for c in range(COIL):
        real = both[BLOCK * c : BLOCK * (c + 1), :LENGTH]
        imag = -both[BLOCK * c : BLOCK * (c + 1), LENGTH:]
        for plane, value in ((c, real), (COIL + c, imag)):
            out[plane] = (kd_ref[plane] + mask * (value - measured[plane])) * scale
            copies.append(pltpu.make_async_copy(out.at[plane], out_hbm.at[plane], sems.at[plane]))
            copies[-1].start()
    for copy in copies:
        copy.wait()


def along_rows(bar, plane, i):
    here = chunk(bar, plane, i)
    below = chunk(bar, plane, i + 1)
    rows = iota((8, LENGTH), 0)
    return jnp.where(rows == 7, pltpu.roll(below, 7, 0), pltpu.roll(here, 7, 0)) - here


def along_cols(bar, plane, i):
    here = chunk(bar, plane, i)
    cols = iota((8, LENGTH), 1)
    return jnp.where(cols == LENGTH - 1, 0.0, pltpu.roll(here, LENGTH - 1, 1) - here)


def project(out, duals, radius, i):
    total = duals[0] * duals[0]
    for value in duals[1:]:
        total += value * value
    scale = jnp.minimum(1.0, radius * lax.rsqrt(total))
    for plane, value in enumerate(duals):
        out[plane, 8 * i : 8 * i + 8, :] = value * scale


def by_frame(run, from_core, from_chip):
    odd = lax.rem(lax.axis_index("tm"), 2)
    pl.when(odd == 0)(lambda: run(from_chip, from_core))
    pl.when(odd == 1)(lambda: run(from_core, from_chip))


def fill_below(bar, n3, first_plane, count):
    row = lax.axis_index("row")
    for plane in range(count):
        place = BLOCK + first_plane + plane
        bar[plane, BLOCK : BLOCK + 1, :] = jnp.where(
            row == ROWS - 1, bar[plane, BLOCK - 1 : BLOCK, :], n3[place : place + 1, 0:LENGTH]
        )


def in_parts(second, pairs, copies, sems):
    for part in range(4):
        rows = pl.ds(16 * part, 16)
        second(2 * part)
        second(2 * part + 1)
        for k, (source, target) in enumerate(pairs):
            copy = pltpu.make_async_copy(source.at[:, rows, :], target.at[:, rows, :], sems.at[4 + 4 * part + k])
            copy.start()
            copies.append(copy)
    for copy in copies:
        copy.wait()


def fields_kernel(
    img, spl, v1, v2, g1, g2, s1, s2, w, q0, from_core, from_chip, z, z_in, n3,
    img_hbm, spl_hbm, v1_hbm, v2_hbm, g1_hbm, g2_hbm, s1_hbm, s2_hbm,
    bar, img_out, spl_out, v1_out, v2_out, g1_out, g2_out, s1_out, s2_out, sems,
):
    keep_time = (lax.axis_index("tm") != lax.axis_size("tm") - 1).astype(F32)
    refs = dict(g1=g1, g2=g2, s1=s1, s2=s2)

    def run(q_in, w_in):
        copies = [
            pltpu.make_async_copy(source, target, sems.at[k])
            for k, (source, target) in enumerate(
                ((img_out, img_hbm), (spl_out, spl_hbm), (v1_out, v1_hbm), (v2_out, v2_hbm))
            )
        ]

        def first(i, carry):
            for reim in range(2):

                def before(f):
                    return chunk(q0, reim, i) if f == 0 else chunk(q_in, 2 * (f - 1) + reim, i)

                values = []
                for field in range(8):
                    plane = 2 * field + reim
                    start = chunk(w, plane, i) if field else chunk(z, reim, i)
                    values.append(start + time_term(before, field))
                    bar[plane, rows_at(8 * i), :] = values[-1]
                img_out[reim, rows_at(8 * i), :] = 0.5 * (values[0] + values[1] + chunk(img, reim, i))
                spl_out[reim, rows_at(8 * i), :] = 0.5 * (values[1] + chunk(spl, reim, i))
                for k in range(3):
                    plane = 2 * k + reim
                    v1_out[plane, rows_at(8 * i), :] = 0.5 * (values[2 + k] + chunk(v1, plane, i))
                    v2_out[plane, rows_at(8 * i), :] = 0.5 * (values[5 + k] + chunk(v2, plane, i))
            return carry

        lax.fori_loop(0, 8, first, 0, unroll=2)
        for copy in copies:
            copy.start()
        fill_below(bar, n3, 0, 16)

        def along_time(field, reim, i):
            plane = 2 * field + reim

            def own(f):
                name, part = TIME_PARTS[f]
                return chunk(refs[name], 2 * part + reim, i)

            ahead = chunk(w_in, plane - 2, i) if field else chunk(z_in, reim, i)
            return ahead + time_term(own, field) - chunk(bar, plane, i)

        def second(i):
            for dual, out, field, beta in ((g1, g1_out, 0, BETA_ONE), (g2, g2_out, 1, BETA_TWO)):
                duals = []
                for k in range(3):
                    for reim in range(2):
                        if k == 0:
                            diff = (beta * keep_time) * along_time(field, reim, i)
                        else:
                            diff = (along_rows, along_cols)[k - 1](bar, 2 * field + reim, i)
                        diff -= chunk(bar, 2 * (2 + 3 * field + k) + reim, i)
                        duals.append(chunk(dual, 2 * k + reim, i) + SIGMA * diff)
                project(out, duals, ALPHA_ONE, i)
            for dual, out, vec, beta in ((s1, s1_out, 2, BETA_ONE), (s2, s2_out, 5, BETA_TWO)):
                duals = [None] * 12
                factor = SIGMA * beta * keep_time
                for reim in range(2):
                    p0, p1, p2 = (2 * (vec + k) + reim for k in range(3))
                    steps = (
                        factor * along_time(vec, reim, i),
                        SIGMA * along_rows(bar, p1, i),
                        SIGMA * along_cols(bar, p2, i),
                        0.5 * SIGMA * along_rows(bar, p0, i) + (0.5 * factor) * along_time(vec + 1, reim, i),
                        0.5 * SIGMA * along_cols(bar, p0, i) + (0.5 * factor) * along_time(vec + 2, reim, i),
                        0.5 * SIGMA * (along_cols(bar, p1, i) + along_rows(bar, p2, i)),
                    )
                    for k, diff in enumerate(steps):
                        duals[2 * k + reim] = chunk(dual, 2 * k + reim, i) + diff
                project(out, duals, ALPHA_ZERO, i)

        pairs = ((g1_out, g1_hbm), (g2_out, g2_hbm), (s1_out, s1_hbm), (s2_out, s2_hbm))
        in_parts(second, pairs, copies, sems)

    by_frame(run, from_core, from_chip)


def shape(*dims):
    return jax.ShapeDtypeStruct(dims, F32)


def call(kernel, outs, ins, cost, in_specs=None, scratch=(), out_space=pltpu.VMEM):
    return pl.pallas_call(
        kernel,
        out_shape=outs,
        in_specs=in_specs or [pl.BlockSpec(memory_space=pltpu.VMEM)] * len(ins),
        out_specs=[pl.BlockSpec(memory_space=out_space)] * len(outs),
        scratch_shapes=list(scratch),
        compiler_params=pltpu.CompilerParams(vmem_limit_bytes=LIMIT),
        cost_estimate=pl.CostEstimate(flops=500 * cost, bytes_accessed=cost, transcendentals=0),
    )(*ins)


def turn(block, distance):
    return lax.ppermute(block, "row", [(i, (i + distance) % ROWS) for i in range(ROWS)])


def body(
    image_now, split_now, vector_one, vector_two, kspace_dual, grad_one, grad_two, sym_one, sym_two,
    measured, sensitivity, sampled,
):
    planes = lambda x: x.reshape(-1, BLOCK, LENGTH)
    img, spl, v1, v2, kd = map(planes, (image_now, split_now, vector_one, vector_two, kspace_dual))
    g1, g2, s1, s2, meas, sens = map(planes, (grad_one, grad_two, sym_one, sym_two, measured, sensitivity))
    first_high, first_low, high, low = map(jnp.asarray, dft_tables())
    frames = lax.axis_size("tm")
    groups = lax.axis_size("coil")
    blocks = (shape(BLOCK, 384), shape(BLOCK + 16, 384), shape(BLOCK, 384), shape(BLOCK, 384))
    hbm = pl.BlockSpec(memory_space=pltpu.HBM)
    a0, a1, a2, a3, mask = call(
        start_kernel, (*blocks, shape(1, LENGTH)),
        [pltpu.with_memory_space_constraint(x, pltpu.HBM) for x in (kd, sampled, first_high, first_low, g1, g2, s1, s2)],
        1,
        in_specs=[hbm] * 8,
        scratch=[
            pltpu.VMEM((2 * COIL, BLOCK, LENGTH), F32), pltpu.VMEM((1, LENGTH), jnp.int32),
            pltpu.VMEM((LENGTH, 2 * LENGTH), BF16), pltpu.VMEM((LENGTH, 2 * LENGTH), BF16),
            pltpu.VMEM((16, 8, LENGTH), F32), pltpu.SemaphoreType.DMA((12,)),
        ],
    )
    b2, b1, b3 = turn(a2, 2), turn(a1, 1), turn(a3, 3)
    after = [(i, i + 1) for i in range(frames - 1)]
    (q_first,) = call(
        pack_kernel, (shape(2 * BLOCK + 16, LENGTH),), (g1, g2, s1, s2, a0), 100_000_000,
        in_specs=[pl.BlockSpec(memory_space=pltpu.VMEM)] * 4 + [pl.BlockSpec(memory_space=pl.ANY)],
    )
    q_first = lax.ppermute(q_first, "tm", after)
    (partial,) = call(combine_kernel, (shape(2, BLOCK, LENGTH),), (a0, b1, b2, b3, high, low, sens), 200_000_000)
    partner = ((1, 0, 3, 2), (3, 2, 1, 0))
    swaps = [
        [(t * groups + c, t * groups + partner[(t + turn) % 2][c]) for t in range(frames) for c in range(groups)]
        for turn in range(2)
    ]
    stack, pair_of = shape(14, BLOCK, LENGTH), shape(2, BLOCK, LENGTH)
    w_out, base, tops, q0, to_core, to_chip = call(
        plain_kernel, (shape(16, BLOCK, LENGTH), pair_of, shape(16, LENGTH), pair_of, stack, stack),
        (img, spl, v1, v2, g1, g2, s1, s2, b1, q_first, partial), 100_000_000,
        in_specs=[pl.BlockSpec(memory_space=pltpu.VMEM)] * 10 + [pl.BlockSpec(memory_space=pl.ANY)],
    )
    received = lax.ppermute(partial, ("tm", "coil"), swaps[0])
    partial, received, w_out = lax.optimization_barrier((partial, received, w_out))
    pair = partial + received
    rest = lax.ppermute(pair, ("tm", "coil"), swaps[1])
    pairs = []
    for t in range(1, frames - 1, 2):
        for c in range(groups):
            there = c if t % 4 == 1 else (c + 1) % groups
            pairs.append((t * groups + c, (t + 1) * groups + there))
            pairs.append(((t + 1) * groups + there, t * groups + c))
    from_chip = lax.ppermute(to_chip, ("tm", "coil"), pairs)
    from_core = lax.ppermute(to_core, "tm", [(t, t ^ 1) for t in range(frames)])
    c_blocks = (shape(BLOCK, 384), shape(BLOCK, 384), shape(BLOCK, 384), shape(BLOCK + 16, 384))
    c0, c1, c2, c3, z = call(
        predict_kernel, (*c_blocks, shape(2, BLOCK, LENGTH)),
        (pair, rest, base, tops, w_out, first_high, first_low, sens), 200_000_000,
    )
    n2, n1, n3 = turn(c2, 2), turn(c1, 1), turn(c3, 3)
    z, from_core = lax.optimization_barrier((z, from_core))
    z_in = lax.ppermute(z, "tm", [(i + 1, i) for i in range(frames - 1)])
    like = lambda x: shape(*x.shape)
    img_new, spl_new, v1_new, v2_new, g1_new, g2_new, s1_new, s2_new = call(
        fields_kernel, tuple(map(like, (img, spl, v1, v2, g1, g2, s1, s2))),
        (img, spl, v1, v2, g1, g2, s1, s2, w_out, q0, from_core, from_chip, z, z_in, n3), 1,
        scratch=[
            pltpu.VMEM((16, BLOCK + 8, LENGTH), F32),
            *(pltpu.VMEM(x.shape, F32) for x in (img, spl, v1, v2, g1, g2, s1, s2)),
            pltpu.SemaphoreType.DMA((20,)),
        ],
        out_space=pltpu.HBM,
    )
    (kspace,) = call(
        finish_kernel, (like(kd),), (c0, n1, n2, n3, high, low, kd, meas, mask), 4_000_000,
        scratch=[pltpu.VMEM(kd.shape, F32), pltpu.SemaphoreType.DMA((2 * COIL,))],
        out_space=pltpu.HBM,
    )
    news = (img_new, spl_new, v1_new, v2_new, kspace, g1_new, g2_new, s1_new, s2_new)
    olds = (image_now, split_now, vector_one, vector_two, kspace_dual, grad_one, grad_two, sym_one, sym_two)
    return tuple(new.reshape(old.shape) for new, old in zip(news, olds))


def solution(mesh):
    image = P(None, "tm", "row", None)
    vector = P(None, None, "tm", "row", None)
    kspace = P(None, "tm", "coil", "row", None)
    return jax.shard_map(
        body,
        mesh=mesh,
        in_specs=(
            image, image, vector, vector, kspace, vector, vector, vector, vector, kspace,
            P(None, "coil", "row", None), P("tm", None),
        ),
        out_specs=(image, image, vector, vector, kspace, vector, vector, vector, vector),
        check_vma=False,
    )
```

```python
import functools
import math

import jax
import jax.numpy as jnp
import ml_dtypes
import numpy as np
from jax import lax
from jax.experimental import pallas as pl
from jax.experimental.pallas import tpu as pltpu
from jax.sharding import PartitionSpec as P

TAU = 0.25
SIGMA = 0.25
LAMBDA_DATA = 2.0
ALPHA_ONE = 2.0
ALPHA_ZERO = 1.2
BETA_ONE = 2.0
BETA_TWO = 0.5

LENGTH = 256
COIL = 3
BLOCK = 64
ROWS = 4
F32 = jnp.float32
BF16 = jnp.bfloat16
LIMIT = 12 * 1024 * 1024


def halves(table):
    high = table.astype(ml_dtypes.bfloat16)
    return high, (table - high.astype(np.float64)).astype(ml_dtypes.bfloat16)


def dft_tables():
    positions = np.arange(LENGTH)
    angles = (positions[:, None] * positions[None, :] % LENGTH) * (2.0 * math.pi / LENGTH)
    real = np.cos(angles) / math.sqrt(LENGTH)
    imag = np.sin(angles) / math.sqrt(LENGTH)
    of_real = np.concatenate([real, imag], axis=1).reshape(ROWS, 1, BLOCK, 2 * LENGTH)
    of_imag = np.concatenate([-imag, real], axis=1).reshape(ROWS, 1, BLOCK, 2 * LENGTH)
    table = np.concatenate([of_real, of_imag], axis=1).reshape(2 * LENGTH, 2 * LENGTH)
    return halves(of_real.reshape(LENGTH, 2 * LENGTH)) + halves(table)


def split(values):
    high = values.astype(BF16)
    return high, (values - high.astype(F32)).astype(BF16)


def dot_nt(a, b):
    return lax.dot_general(a, b, (((1,), (1,)), ((), ())), preferred_element_type=F32)


def dot_nn(a, b):
    return lax.dot_general(a, b, (((1,), (0,)), ((), ())), preferred_element_type=F32)


def first_transform(table_high, table_low, right, row):
    def blocks(ref):
        return jnp.concatenate(
            [ref[pl.ds(pl.multiple_of(lax.rem(row + d, ROWS) * BLOCK, BLOCK), BLOCK), :] for d in range(ROWS)], axis=0
        )

    high, low = split(right)
    left_high = blocks(table_high)
    return dot_nt(left_high, high) + (dot_nt(left_high, low) + dot_nt(blocks(table_low), high))


def second_transform(table_high, table_low, received, row):
    def blocks(ref):
        return jnp.concatenate(
            [ref[pl.ds(pl.multiple_of(lax.rem(row + ROWS - d, ROWS) * 128, 128), 128), :] for d in range(ROWS)], axis=0
        )

    left = jnp.concatenate(
        [
            jnp.concatenate([block[:BLOCK, 128 * c : 128 * (c + 1)] for block in received], axis=1)
            for c in range(COIL)
        ],
        axis=0,
    )
    high, low = split(left)
    right_high = blocks(table_high)
    return dot_nn(high, right_high) + (dot_nn(low, right_high) + dot_nn(high, blocks(table_low)))


def iota(shape, dimension):
    return lax.broadcasted_iota(jnp.int32, shape, dimension)


ROW_PARTS = (("g1", 1), ("g2", 1), ("s1", 1), ("s1", 3), ("s1", 5), ("s2", 1), ("s2", 3), ("s2", 5))
TIME_PARTS = (("g1", 0), ("g2", 0), ("s1", 0), ("s1", 3), ("s1", 4), ("s2", 0), ("s2", 3), ("s2", 4))


def start_kernel(
    kd_hbm, lines_hbm, th_hbm, tl_hbm, g1, g2, s1, s2, o0, o1, o2, o3, mask_out,
    kd_ref, lines_ref, th_ref, tl_ref, ends, sems
):
    row = lax.axis_index("row")
    copies = [
        pltpu.make_async_copy(source, target, sems.at[k])
        for k, (source, target) in enumerate(
            ((kd_hbm, kd_ref), (lines_hbm, lines_ref), (th_hbm, th_ref), (tl_hbm, tl_ref))
        )
    ]
    refs = dict(g1=g1, g2=g2, s1=s1, s2=s2)
    for index, (name, part) in enumerate(ROW_PARTS):
        copies.append(
            pltpu.make_async_copy(
                refs[name].at[2 * part : 2 * part + 2, BLOCK - 8 : BLOCK, :],
                ends.at[2 * index : 2 * index + 2],
                sems.at[4 + index],
            )
        )
    for copy in copies:
        copy.start()
    for copy in copies[:4]:
        copy.wait()
    mask = lines_ref[...].astype(F32)
    mask_out[...] = mask
    parts = []
    for c in range(COIL):
        real = kd_ref[c] * mask
        imag = kd_ref[COIL + c] * mask
        parts.append(jnp.concatenate([real, -imag], axis=1))
        parts.append(jnp.concatenate([imag, real], axis=1))
    out = first_transform(th_ref, tl_ref, jnp.concatenate(parts, axis=0), row)
    for d, ref in enumerate((o0, o1, o2, o3)):
        ref[0:BLOCK, :] = out[BLOCK * d : BLOCK * (d + 1)]
    for copy in copies[4:]:
        copy.wait()
    o1[BLOCK:, LENGTH:] = jnp.zeros((16, 128), F32)
    for plane in range(16):
        o1[BLOCK + plane : BLOCK + plane + 1, 0:LENGTH] = ends[plane, 7:8, :]


def rows_at(start):
    return pl.ds(start if isinstance(start, int) else pl.multiple_of(start, 8), 8)


def chunk(ref, plane, i):
    return ref[plane, rows_at(i * 8), :]


def pack_kernel(g1, g2, s1, s2, order, q_first):
    refs = dict(g1=g1, g2=g2, s1=s1, s2=s2)
    for reim in range(2):
        q_first[BLOCK * reim : BLOCK * (reim + 1), :] = g1[reim]
        tops = [refs[name][2 * part + reim, 0:1, :] for name, part in TIME_PARTS]
        for field in range(8):
            place = 2 * BLOCK + 2 * field + reim
            q_first[place : place + 1, :] = time_term(lambda k: tops[k], field)


def plain_kernel(img, spl, v1, v2, g1, g2, s1, s2, b1, q_first, order, w_out, image_out, tops, q0_out, to_core, to_chip):
    odd = lax.rem(lax.axis_index("tm"), 2)
    row = lax.axis_index("row")
    keep_time = (lax.axis_index("tm") != lax.axis_size("tm") - 1).astype(F32)
    refs = dict(g1=g1, g2=g2, s1=s1, s2=s2)
    edge = jnp.where(row == 0, 0.0, b1[BLOCK:, 0:LENGTH])
    where = {part: 2 * index for index, part in enumerate(ROW_PARTS)}

    def step(i, carry):
        rows = iota((8, LENGTH), 0)
        cols = iota((8, LENGTH), 1)
        drop_row = (rows == 7) & (i == 7) & (row == ROWS - 1)

        def adj_rows(name, plane):
            ref = refs[name]
            here = chunk(ref, plane, i)
            above = chunk(ref, plane, jnp.maximum(i - 1, 0))
            at = where[name, plane // 2] + plane % 2
            above = jnp.where(i == 0, edge[at : at + 1], above)
            behind = jnp.where(rows == 0, pltpu.roll(above, 1, 0), pltpu.roll(here, 1, 0))
            return behind - jnp.where(drop_row, 0.0, here)

        def adj_cols(ref, plane):
            here = chunk(ref, plane, i)
            behind = jnp.where(cols == 0, 0.0, pltpu.roll(here, 1, 1))
            return behind - jnp.where(cols == LENGTH - 1, 0.0, here)

        def put(ref, plane, value):
            ref[plane, pl.ds(pl.multiple_of(i * 8, 8), 8), :] = value

        for reim in range(2):
            z, y, x = reim, 2 + reim, 4 + reim
            one = -BETA_ONE * keep_time * chunk(g1, z, i) + adj_rows("g1", y) + adj_cols(g1, x)
            two = -BETA_TWO * keep_time * chunk(g2, z, i) + adj_rows("g2", y) + adj_cols(g2, x)
            image = chunk(img, reim, i) - 2.0 * TAU * one
            other = chunk(spl, reim, i) - 2.0 * TAU * (two - one)
            before = q_first[pl.ds(pl.multiple_of(BLOCK * reim + i * 8, 8), 8), :]
            put(q0_out, reim, before)
            put(image_out, reim, image - 2.0 * TAU * BETA_ONE * before)
            put(w_out, reim, image - other)
            put(w_out, 2 + reim, other)
            for base, vec, grad, name, beta in ((4, v1, g1, "s1", BETA_ONE), (10, v2, g2, "s2", BETA_TWO)):
                sym = refs[name]
                p0, p1, p2, p3, p4, p5 = (2 * k + reim for k in range(6))
                first = -beta * keep_time * chunk(sym, p0, i) + 0.5 * (adj_rows(name, p3) + adj_cols(sym, p4))
                second = adj_rows(name, p1) - 0.5 * beta * keep_time * chunk(sym, p3, i) + 0.5 * adj_cols(sym, p5)
                third = adj_cols(sym, p2) - 0.5 * beta * keep_time * chunk(sym, p4, i) + 0.5 * adj_rows(name, p5)
                for k, adjoint in enumerate((first, second, third)):
                    value = chunk(vec, 2 * k + reim, i) - 2.0 * TAU * (adjoint - chunk(grad, 2 * k + reim, i))
                    put(w_out, base + 2 * k + reim, value)
        return carry

    lax.fori_loop(0, 8, step, 0)
    for plane in range(16):
        place = 2 * BLOCK + plane
        tops[plane : plane + 1, :] = w_out[plane, 0:1, :] + q_first[place : place + 1, :]

    def messages(q_to, w_to):
        for index, (name, part) in enumerate(TIME_PARTS[1:]):
            q_to[2 * index : 2 * index + 2] = refs[name][2 * part : 2 * part + 2]
        w_to[...] = w_out[2:]

    pl.when(odd == 0)(lambda: messages(to_core, to_chip))
    pl.when(odd == 1)(lambda: messages(to_chip, to_core))


def combine_kernel(b0, b1, b2, b3, th_ref, tl_ref, sens, out):
    row = lax.axis_index("row")
    both = second_transform(th_ref, tl_ref, (b0, b1, b2, b3), row)
    real_sum = None
    for c in range(COIL):
        real = both[BLOCK * c : BLOCK * (c + 1), :LENGTH]
        imag = both[BLOCK * c : BLOCK * (c + 1), LENGTH:]
        real_term = sens[c] * real + sens[COIL + c] * imag
        imag_term = sens[c] * imag - sens[COIL + c] * real
        real_sum = real_term if real_sum is None else real_sum + real_term
        imag_sum = imag_term if c == 0 else imag_sum + imag_term
    out[0] = real_sum
    out[1] = imag_sum


def time_term(q, field):
    if field == 0:
        return -2.0 * TAU * (2.0 * BETA_ONE * q(0) - BETA_TWO * q(1))
    if field == 1:
        return -2.0 * TAU * (BETA_TWO * q(1) - BETA_ONE * q(0))
    beta = BETA_ONE if field < 5 else BETA_TWO
    return (-2.0 * TAU * beta * (1.0 if field in (2, 5) else 0.5)) * q(field)


def predict_kernel(sum_a, sum_b, base, tops, w, th_ref, tl_ref, sens, o0, o1, o2, o3, z_out):
    row = lax.axis_index("row")
    image = []
    for reim in range(2):
        back = sum_a[reim] + sum_b[reim]
        z_out[reim] = w[reim] - 2.0 * TAU * back
        image.append(base[reim] - 2.0 * TAU * back)
    parts = []
    for c in range(COIL):
        real = sens[c] * image[0] - sens[COIL + c] * image[1]
        imag = sens[c] * image[1] + sens[COIL + c] * image[0]
        parts.append(jnp.concatenate([real, imag], axis=1))
        parts.append(jnp.concatenate([-imag, real], axis=1))
    out = first_transform(th_ref, tl_ref, jnp.concatenate(parts, axis=0), row)
    for d, ref in enumerate((o0, o1, o2, o3)):
        ref[0:BLOCK, :] = out[BLOCK * d : BLOCK * (d + 1)]
    o3[BLOCK:, LENGTH:] = jnp.zeros((16, 128), F32)
    o3[BLOCK:, 0:LENGTH] = tops[...]
    for reim in range(2):
        o3[BLOCK + reim : BLOCK + reim + 1, 0:LENGTH] -= 2.0 * TAU * (sum_a[reim, 0:1, :] + sum_b[reim, 0:1, :])


def finish_kernel(b0, b1, b2, b3, th_ref, tl_ref, kd_ref, measured, mask_ref, out_hbm, out, sems):
    row = lax.axis_index("row")
    both = second_transform(th_ref, tl_ref, (b0, b1, b2, b3), row)
    mask = SIGMA * mask_ref[...]
    scale = 1.0 / (1.0 + SIGMA / LAMBDA_DATA)
    copies = []
    for c in range(COIL):
        real = both[BLOCK * c : BLOCK * (c + 1), :LENGTH]
        imag = -both[BLOCK * c : BLOCK * (c + 1), LENGTH:]
        for plane, value in ((c, real), (COIL + c, imag)):
            out[plane] = (kd_ref[plane] + mask * (value - measured[plane])) * scale
            copies.append(pltpu.make_async_copy(out.at[plane], out_hbm.at[plane], sems.at[plane]))
            copies[-1].start()
    for copy in copies:
        copy.wait()


def along_rows(bar, plane, i):
    here = chunk(bar, plane, i)
    below = chunk(bar, plane, i + 1)
    rows = iota((8, LENGTH), 0)
    return jnp.where(rows == 7, pltpu.roll(below, 7, 0), pltpu.roll(here, 7, 0)) - here


def along_cols(bar, plane, i):
    here = chunk(bar, plane, i)
    cols = iota((8, LENGTH), 1)
    return jnp.where(cols == LENGTH - 1, 0.0, pltpu.roll(here, LENGTH - 1, 1) - here)


def project(out, duals, radius, i):
    total = duals[0] * duals[0]
    for value in duals[1:]:
        total += value * value
    scale = jnp.minimum(1.0, radius * lax.rsqrt(total))
    for plane, value in enumerate(duals):
        out[plane, 8 * i : 8 * i + 8, :] = value * scale


def by_frame(run, from_core, from_chip):
    odd = lax.rem(lax.axis_index("tm"), 2)
    pl.when(odd == 0)(lambda: run(from_chip, from_core))
    pl.when(odd == 1)(lambda: run(from_core, from_chip))


def fill_below(bar, n3, first_plane, count):
    row = lax.axis_index("row")
    for plane in range(count):
        place = BLOCK + first_plane + plane
        bar[plane, BLOCK : BLOCK + 1, :] = jnp.where(
            row == ROWS - 1, bar[plane, BLOCK - 1 : BLOCK, :], n3[place : place + 1, 0:LENGTH]
        )


def in_parts(second, pairs, copies, sems):
    for part in range(4):
        rows = pl.ds(16 * part, 16)
        second(2 * part)
        second(2 * part + 1)
        for k, (source, target) in enumerate(pairs):
            copy = pltpu.make_async_copy(source.at[:, rows, :], target.at[:, rows, :], sems.at[4 + 4 * part + k])
            copy.start()
            copies.append(copy)
    for copy in copies:
        copy.wait()


def fields_kernel(
    img, spl, v1, v2, g1, g2, s1, s2, w, q0, from_core, from_chip, z, z_in, n3,
    img_hbm, spl_hbm, v1_hbm, v2_hbm, g1_hbm, g2_hbm, s1_hbm, s2_hbm,
    bar, img_out, spl_out, v1_out, v2_out, g1_out, g2_out, s1_out, s2_out, sems,
):
    keep_time = (lax.axis_index("tm") != lax.axis_size("tm") - 1).astype(F32)
    refs = dict(g1=g1, g2=g2, s1=s1, s2=s2)

    def run(q_in, w_in):
        copies = [
            pltpu.make_async_copy(source, target, sems.at[k])
            for k, (source, target) in enumerate(
                ((img_out, img_hbm), (spl_out, spl_hbm), (v1_out, v1_hbm), (v2_out, v2_hbm))
            )
        ]

        def first(i, carry):
            for reim in range(2):

                def before(f):
                    return chunk(q0, reim, i) if f == 0 else chunk(q_in, 2 * (f - 1) + reim, i)

                values = []
                for field in range(8):
                    plane = 2 * field + reim
                    start = chunk(w, plane, i) if field else chunk(z, reim, i)
                    values.append(start + time_term(before, field))
                    bar[plane, rows_at(8 * i), :] = values[-1]
                img_out[reim, rows_at(8 * i), :] = 0.5 * (values[0] + values[1] + chunk(img, reim, i))
                spl_out[reim, rows_at(8 * i), :] = 0.5 * (values[1] + chunk(spl, reim, i))
                for k in range(3):
                    plane = 2 * k + reim
                    v1_out[plane, rows_at(8 * i), :] = 0.5 * (values[2 + k] + chunk(v1, plane, i))
                    v2_out[plane, rows_at(8 * i), :] = 0.5 * (values[5 + k] + chunk(v2, plane, i))
            return carry

        lax.fori_loop(0, 8, first, 0, unroll=2)
        for copy in copies:
            copy.start()
        fill_below(bar, n3, 0, 16)

        def along_time(field, reim, i):
            plane = 2 * field + reim

            def own(f):
                name, part = TIME_PARTS[f]
                return chunk(refs[name], 2 * part + reim, i)

            ahead = chunk(w_in, plane - 2, i) if field else chunk(z_in, reim, i)
            return ahead + time_term(own, field) - chunk(bar, plane, i)

        def second(i):
            for dual, out, field, beta in ((g1, g1_out, 0, BETA_ONE), (g2, g2_out, 1, BETA_TWO)):
                duals = []
                for k in range(3):
                    for reim in range(2):
                        if k == 0:
                            diff = (beta * keep_time) * along_time(field, reim, i)
                        else:
                            diff = (along_rows, along_cols)[k - 1](bar, 2 * field + reim, i)
                        diff -= chunk(bar, 2 * (2 + 3 * field + k) + reim, i)
                        duals.append(chunk(dual, 2 * k + reim, i) + SIGMA * diff)
                project(out, duals, ALPHA_ONE, i)
            for dual, out, vec, beta in ((s1, s1_out, 2, BETA_ONE), (s2, s2_out, 5, BETA_TWO)):
                duals = [None] * 12
                factor = SIGMA * beta * keep_time
                for reim in range(2):
                    p0, p1, p2 = (2 * (vec + k) + reim for k in range(3))
                    steps = (
                        factor * along_time(vec, reim, i),
                        SIGMA * along_rows(bar, p1, i),
                        SIGMA * along_cols(bar, p2, i),
                        0.5 * SIGMA * along_rows(bar, p0, i) + (0.5 * factor) * along_time(vec + 1, reim, i),
                        0.5 * SIGMA * along_cols(bar, p0, i) + (0.5 * factor) * along_time(vec + 2, reim, i),
                        0.5 * SIGMA * (along_cols(bar, p1, i) + along_rows(bar, p2, i)),
                    )
                    for k, diff in enumerate(steps):
                        duals[2 * k + reim] = chunk(dual, 2 * k + reim, i) + diff
                project(out, duals, ALPHA_ZERO, i)

        pairs = ((g1_out, g1_hbm), (g2_out, g2_hbm), (s1_out, s1_hbm), (s2_out, s2_hbm))
        in_parts(second, pairs, copies, sems)

    by_frame(run, from_core, from_chip)


def shape(*dims):
    return jax.ShapeDtypeStruct(dims, F32)


def call(kernel, outs, ins, cost, in_specs=None, scratch=(), out_space=pltpu.VMEM):
    return pl.pallas_call(
        kernel,
        out_shape=outs,
        in_specs=in_specs or [pl.BlockSpec(memory_space=pltpu.VMEM)] * len(ins),
        out_specs=[pl.BlockSpec(memory_space=out_space)] * len(outs),
        scratch_shapes=list(scratch),
        compiler_params=pltpu.CompilerParams(vmem_limit_bytes=LIMIT),
        cost_estimate=pl.CostEstimate(flops=500 * cost, bytes_accessed=cost, transcendentals=0),
    )(*ins)


def turn(block, distance):
    return lax.ppermute(block, "row", [(i, (i + distance) % ROWS) for i in range(ROWS)])


def body(
    image_now, split_now, vector_one, vector_two, kspace_dual, grad_one, grad_two, sym_one, sym_two,
    measured, sensitivity, sampled,
):
    planes = lambda x: x.reshape(-1, BLOCK, LENGTH)
    img, spl, v1, v2, kd = map(planes, (image_now, split_now, vector_one, vector_two, kspace_dual))
    g1, g2, s1, s2, meas, sens = map(planes, (grad_one, grad_two, sym_one, sym_two, measured, sensitivity))
    first_high, first_low, high, low = map(jnp.asarray, dft_tables())
    frames = lax.axis_size("tm")
    groups = lax.axis_size("coil")
    blocks = (shape(BLOCK, 384), shape(BLOCK + 16, 384), shape(BLOCK, 384), shape(BLOCK, 384))
    hbm = pl.BlockSpec(memory_space=pltpu.HBM)
    a0, a1, a2, a3, mask = call(
        start_kernel, (*blocks, shape(1, LENGTH)),
        [pltpu.with_memory_space_constraint(x, pltpu.HBM) for x in (kd, sampled, first_high, first_low, g1, g2, s1, s2)],
        1,
        in_specs=[hbm] * 8,
        scratch=[
            pltpu.VMEM((2 * COIL, BLOCK, LENGTH), F32), pltpu.VMEM((1, LENGTH), jnp.int32),
            pltpu.VMEM((LENGTH, 2 * LENGTH), BF16), pltpu.VMEM((LENGTH, 2 * LENGTH), BF16),
            pltpu.VMEM((16, 8, LENGTH), F32), pltpu.SemaphoreType.DMA((12,)),
        ],
    )
    b2, b1, b3 = turn(a2, 2), turn(a1, 1), turn(a3, 3)
    after = [(i, i + 1) for i in range(frames - 1)]
    (q_first,) = call(
        pack_kernel, (shape(2 * BLOCK + 16, LENGTH),), (g1, g2, s1, s2, a0), 100_000_000,
        in_specs=[pl.BlockSpec(memory_space=pltpu.VMEM)] * 4 + [pl.BlockSpec(memory_space=pl.ANY)],
    )
    q_first = lax.ppermute(q_first, "tm", after)
    (partial,) = call(combine_kernel, (shape(2, BLOCK, LENGTH),), (a0, b1, b2, b3, high, low, sens), 200_000_000)
    partner = ((1, 0, 3, 2), (3, 2, 1, 0))
    swaps = [
        [(t * groups + c, t * groups + partner[(t + turn) % 2][c]) for t in range(frames) for c in range(groups)]
        for turn in range(2)
    ]
    stack, pair_of = shape(14, BLOCK, LENGTH), shape(2, BLOCK, LENGTH)
    w_out, base, tops, q0, to_core, to_chip = call(
        plain_kernel, (shape(16, BLOCK, LENGTH), pair_of, shape(16, LENGTH), pair_of, stack, stack),
        (img, spl, v1, v2, g1, g2, s1, s2, b1, q_first, partial), 100_000_000,
        in_specs=[pl.BlockSpec(memory_space=pltpu.VMEM)] * 10 + [pl.BlockSpec(memory_space=pl.ANY)],
    )
    received = lax.ppermute(partial, ("tm", "coil"), swaps[0])
    partial, received, w_out = lax.optimization_barrier((partial, received, w_out))
    pair = partial + received
    rest = lax.ppermute(pair, ("tm", "coil"), swaps[1])
    pairs = []
    for t in range(1, frames - 1, 2):
        for c in range(groups):
            there = c if t % 4 == 1 else (c + 1) % groups
            pairs.append((t * groups + c, (t + 1) * groups + there))
            pairs.append(((t + 1) * groups + there, t * groups + c))
    from_chip = lax.ppermute(to_chip, ("tm", "coil"), pairs)
    to_core, rest = lax.optimization_barrier((to_core, rest))
    from_core = lax.ppermute(to_core, "tm", [(t, t ^ 1) for t in range(frames)])
    c_blocks = (shape(BLOCK, 384), shape(BLOCK, 384), shape(BLOCK, 384), shape(BLOCK + 16, 384))
    c0, c1, c2, c3, z = call(
        predict_kernel, (*c_blocks, shape(2, BLOCK, LENGTH)),
        (pair, rest, base, tops, w_out, first_high, first_low, sens), 200_000_000,
    )
    n2, n1, n3 = turn(c2, 2), turn(c1, 1), turn(c3, 3)
    z, from_core = lax.optimization_barrier((z, from_core))
    z_in = lax.ppermute(z, "tm", [(i + 1, i) for i in range(frames - 1)])
    like = lambda x: shape(*x.shape)
    img_new, spl_new, v1_new, v2_new, g1_new, g2_new, s1_new, s2_new = call(
        fields_kernel, tuple(map(like, (img, spl, v1, v2, g1, g2, s1, s2))),
        (img, spl, v1, v2, g1, g2, s1, s2, w_out, q0, from_core, from_chip, z, z_in, n3), 1,
        scratch=[
            pltpu.VMEM((16, BLOCK + 8, LENGTH), F32),
            *(pltpu.VMEM(x.shape, F32) for x in (img, spl, v1, v2, g1, g2, s1, s2)),
            pltpu.SemaphoreType.DMA((20,)),
        ],
        out_space=pltpu.HBM,
    )
    (kspace,) = call(
        finish_kernel, (like(kd),), (c0, n1, n2, n3, high, low, kd, meas, mask), 4_000_000,
        scratch=[pltpu.VMEM(kd.shape, F32), pltpu.SemaphoreType.DMA((2 * COIL,))],
        out_space=pltpu.HBM,
    )
    news = (img_new, spl_new, v1_new, v2_new, kspace, g1_new, g2_new, s1_new, s2_new)
    olds = (image_now, split_now, vector_one, vector_two, kspace_dual, grad_one, grad_two, sym_one, sym_two)
    return tuple(new.reshape(old.shape) for new, old in zip(news, olds))


def solution(mesh):
    image = P(None, "tm", "row", None)
    vector = P(None, None, "tm", "row", None)
    kspace = P(None, "tm", "coil", "row", None)
    return jax.shard_map(
        body,
        mesh=mesh,
        in_specs=(
            image, image, vector, vector, kspace, vector, vector, vector, vector, kspace,
            P(None, "coil", "row", None), P("tm", None),
        ),
        out_specs=(image, image, vector, vector, kspace, vector, vector, vector, vector),
        check_vma=False,
    )
```

```python
import functools
import math

import jax
import jax.numpy as jnp
import ml_dtypes
import numpy as np
from jax import lax
from jax.experimental import pallas as pl
from jax.experimental.pallas import tpu as pltpu
from jax.sharding import PartitionSpec as P

TAU = 0.25
SIGMA = 0.25
LAMBDA_DATA = 2.0
ALPHA_ONE = 2.0
ALPHA_ZERO = 1.2
BETA_ONE = 2.0
BETA_TWO = 0.5

LENGTH = 256
COIL = 3
BLOCK = 64
ROWS = 4
F32 = jnp.float32
BF16 = jnp.bfloat16
LIMIT = 12 * 1024 * 1024


def halves(table):
    high = table.astype(ml_dtypes.bfloat16)
    return high, (table - high.astype(np.float64)).astype(ml_dtypes.bfloat16)


def dft_tables():
    positions = np.arange(LENGTH)
    angles = (positions[:, None] * positions[None, :] % LENGTH) * (2.0 * math.pi / LENGTH)
    real = np.cos(angles) / math.sqrt(LENGTH)
    imag = np.sin(angles) / math.sqrt(LENGTH)
    of_real = np.concatenate([real, imag], axis=1).reshape(ROWS, 1, BLOCK, 2 * LENGTH)
    of_imag = np.concatenate([-imag, real], axis=1).reshape(ROWS, 1, BLOCK, 2 * LENGTH)
    table = np.concatenate([of_real, of_imag], axis=1).reshape(2 * LENGTH, 2 * LENGTH)
    return halves(of_real.reshape(LENGTH, 2 * LENGTH)) + halves(table)


def split(values):
    high = values.astype(BF16)
    return high, (values - high.astype(F32)).astype(BF16)


def dot_nt(a, b):
    return lax.dot_general(a, b, (((1,), (1,)), ((), ())), preferred_element_type=F32)


def dot_nn(a, b):
    return lax.dot_general(a, b, (((1,), (0,)), ((), ())), preferred_element_type=F32)


def first_transform(table_high, table_low, right, row):
    def blocks(ref):
        return jnp.concatenate(
            [ref[pl.ds(pl.multiple_of(lax.rem(row + d, ROWS) * BLOCK, BLOCK), BLOCK), :] for d in range(ROWS)], axis=0
        )

    high, low = split(right)
    left_high = blocks(table_high)
    return dot_nt(left_high, high) + (dot_nt(left_high, low) + dot_nt(blocks(table_low), high))


def second_transform(table_high, table_low, received, row):
    def blocks(ref):
        return jnp.concatenate(
            [ref[pl.ds(pl.multiple_of(lax.rem(row + ROWS - d, ROWS) * 128, 128), 128), :] for d in range(ROWS)], axis=0
        )

    left = jnp.concatenate(
        [
            jnp.concatenate([block[:BLOCK, 128 * c : 128 * (c + 1)] for block in received], axis=1)
            for c in range(COIL)
        ],
        axis=0,
    )
    high, low = split(left)
    right_high = blocks(table_high)
    return dot_nn(high, right_high) + (dot_nn(low, right_high) + dot_nn(high, blocks(table_low)))


def iota(shape, dimension):
    return lax.broadcasted_iota(jnp.int32, shape, dimension)


ROW_PARTS = (("g1", 1), ("g2", 1), ("s1", 1), ("s1", 3), ("s1", 5), ("s2", 1), ("s2", 3), ("s2", 5))
TIME_PARTS = (("g1", 0), ("g2", 0), ("s1", 0), ("s1", 3), ("s1", 4), ("s2", 0), ("s2", 3), ("s2", 4))


def start_kernel(
    kd_hbm, lines_hbm, th_hbm, tl_hbm, g1, g2, s1, s2, o0, o1, o2, o3, mask_out,
    kd_ref, lines_ref, th_ref, tl_ref, ends, sems
):
    row = lax.axis_index("row")
    copies = [
        pltpu.make_async_copy(source, target, sems.at[k])
        for k, (source, target) in enumerate(
            ((kd_hbm, kd_ref), (lines_hbm, lines_ref), (th_hbm, th_ref), (tl_hbm, tl_ref))
        )
    ]
    refs = dict(g1=g1, g2=g2, s1=s1, s2=s2)
    for index, (name, part) in enumerate(ROW_PARTS):
        copies.append(
            pltpu.make_async_copy(
                refs[name].at[2 * part : 2 * part + 2, BLOCK - 8 : BLOCK, :],
                ends.at[2 * index : 2 * index + 2],
                sems.at[4 + index],
            )
        )
    for copy in copies:
        copy.start()
    for copy in copies[:4]:
        copy.wait()
    mask = lines_ref[...].astype(F32)
    mask_out[...] = mask
    parts = []
    for c in range(COIL):
        real = kd_ref[c] * mask
        imag = kd_ref[COIL + c] * mask
        parts.append(jnp.concatenate([real, -imag], axis=1))
        parts.append(jnp.concatenate([imag, real], axis=1))
    out = first_transform(th_ref, tl_ref, jnp.concatenate(parts, axis=0), row)
    for d, ref in enumerate((o0, o1, o2, o3)):
        ref[0:BLOCK, :] = out[BLOCK * d : BLOCK * (d + 1)]
    for copy in copies[4:]:
        copy.wait()
    o1[BLOCK:, LENGTH:] = jnp.zeros((16, 128), F32)
    o2[BLOCK:, :] = jnp.zeros((24, 384), F32)
    for plane in range(16):
        o1[BLOCK + plane : BLOCK + plane + 1, 0:LENGTH] = ends[plane, 7:8, :]


def rows_at(start):
    return pl.ds(start if isinstance(start, int) else pl.multiple_of(start, 8), 8)


def chunk(ref, plane, i):
    return ref[plane, rows_at(i * 8), :]


def pack_kernel(g1, g2, s1, s2, order, q_first):
    refs = dict(g1=g1, g2=g2, s1=s1, s2=s2)
    for reim in range(2):
        q_first[BLOCK * reim : BLOCK * (reim + 1), :] = g1[reim]
        tops = [refs[name][2 * part + reim, 0:1, :] for name, part in TIME_PARTS]
        for field in range(8):
            place = 2 * BLOCK + 2 * field + reim
            q_first[place : place + 1, :] = time_term(lambda k: tops[k], field)


def plain_kernel(img, spl, v1, v2, g1, g2, s1, s2, b1, q_first, order, w_out, image_out, tops, q0_out, to_core, to_chip):
    odd = lax.rem(lax.axis_index("tm"), 2)
    row = lax.axis_index("row")
    keep_time = (lax.axis_index("tm") != lax.axis_size("tm") - 1).astype(F32)
    refs = dict(g1=g1, g2=g2, s1=s1, s2=s2)
    edge = jnp.where(row == 0, 0.0, b1[BLOCK:, 0:LENGTH])
    where = {part: 2 * index for index, part in enumerate(ROW_PARTS)}

    def step(i, carry):
        rows = iota((8, LENGTH), 0)
        cols = iota((8, LENGTH), 1)
        drop_row = (rows == 7) & (i == 7) & (row == ROWS - 1)

        def adj_rows(name, plane):
            ref = refs[name]
            here = chunk(ref, plane, i)
            above = chunk(ref, plane, jnp.maximum(i - 1, 0))
            at = where[name, plane // 2] + plane % 2
            above = jnp.where(i == 0, edge[at : at + 1], above)
            behind = jnp.where(rows == 0, pltpu.roll(above, 1, 0), pltpu.roll(here, 1, 0))
            return behind - jnp.where(drop_row, 0.0, here)

        def adj_cols(ref, plane):
            here = chunk(ref, plane, i)
            behind = jnp.where(cols == 0, 0.0, pltpu.roll(here, 1, 1))
            return behind - jnp.where(cols == LENGTH - 1, 0.0, here)

        def put(ref, plane, value):
            ref[plane, pl.ds(pl.multiple_of(i * 8, 8), 8), :] = value

        for reim in range(2):
            z, y, x = reim, 2 + reim, 4 + reim
            one = -BETA_ONE * keep_time * chunk(g1, z, i) + adj_rows("g1", y) + adj_cols(g1, x)
            two = -BETA_TWO * keep_time * chunk(g2, z, i) + adj_rows("g2", y) + adj_cols(g2, x)
            image = chunk(img, reim, i) - 2.0 * TAU * one
            other = chunk(spl, reim, i) - 2.0 * TAU * (two - one)
            before = q_first[pl.ds(pl.multiple_of(BLOCK * reim + i * 8, 8), 8), :]
            put(q0_out, reim, before)
            put(image_out, reim, image - 2.0 * TAU * BETA_ONE * before)
            put(w_out, reim, image - other)
            put(w_out, 2 + reim, other)
            for base, vec, grad, name, beta in ((4, v1, g1, "s1", BETA_ONE), (10, v2, g2, "s2", BETA_TWO)):
                sym = refs[name]
                p0, p1, p2, p3, p4, p5 = (2 * k + reim for k in range(6))
                first = -beta * keep_time * chunk(sym, p0, i) + 0.5 * (adj_rows(name, p3) + adj_cols(sym, p4))
                second = adj_rows(name, p1) - 0.5 * beta * keep_time * chunk(sym, p3, i) + 0.5 * adj_cols(sym, p5)
                third = adj_cols(sym, p2) - 0.5 * beta * keep_time * chunk(sym, p4, i) + 0.5 * adj_rows(name, p5)
                for k, adjoint in enumerate((first, second, third)):
                    value = chunk(vec, 2 * k + reim, i) - 2.0 * TAU * (adjoint - chunk(grad, 2 * k + reim, i))
                    put(w_out, base + 2 * k + reim, value)
        return carry

    lax.fori_loop(0, 8, step, 0)
    for plane in range(16):
        place = 2 * BLOCK + plane
        tops[plane : plane + 1, :] = w_out[plane, 0:1, :] + q_first[place : place + 1, :]

    def messages(q_to, w_to):
        for index, (name, part) in enumerate(TIME_PARTS[1:]):
            q_to[2 * index : 2 * index + 2] = refs[name][2 * part : 2 * part + 2]
        w_to[...] = w_out[2:]

    pl.when(odd == 0)(lambda: messages(to_core, to_chip))
    pl.when(odd == 1)(lambda: messages(to_chip, to_core))


def combine_kernel(b0, b1, b2, b3, th_ref, tl_ref, sens, out):
    row = lax.axis_index("row")
    both = second_transform(th_ref, tl_ref, (b0, b1, b2, b3), row)
    real_sum = None
    for c in range(COIL):
        real = both[BLOCK * c : BLOCK * (c + 1), :LENGTH]
        imag = both[BLOCK * c : BLOCK * (c + 1), LENGTH:]
        real_term = sens[c] * real + sens[COIL + c] * imag
        imag_term = sens[c] * imag - sens[COIL + c] * real
        real_sum = real_term if real_sum is None else real_sum + real_term
        imag_sum = imag_term if c == 0 else imag_sum + imag_term
    out[0] = real_sum
    out[1] = imag_sum


def time_term(q, field):
    if field == 0:
        return -2.0 * TAU * (2.0 * BETA_ONE * q(0) - BETA_TWO * q(1))
    if field == 1:
        return -2.0 * TAU * (BETA_TWO * q(1) - BETA_ONE * q(0))
    beta = BETA_ONE if field < 5 else BETA_TWO
    return (-2.0 * TAU * beta * (1.0 if field in (2, 5) else 0.5)) * q(field)


def predict_kernel(sum_a, sum_b, base, tops, w, th_ref, tl_ref, sens, o0, o1, o2, o3, z_out):
    row = lax.axis_index("row")
    image = []
    for reim in range(2):
        back = sum_a[reim] + sum_b[reim]
        z_out[reim] = w[reim] - 2.0 * TAU * back
        image.append(base[reim] - 2.0 * TAU * back)
    parts = []
    for c in range(COIL):
        real = sens[c] * image[0] - sens[COIL + c] * image[1]
        imag = sens[c] * image[1] + sens[COIL + c] * image[0]
        parts.append(jnp.concatenate([real, imag], axis=1))
        parts.append(jnp.concatenate([-imag, real], axis=1))
    out = first_transform(th_ref, tl_ref, jnp.concatenate(parts, axis=0), row)
    for d, ref in enumerate((o0, o1, o2, o3)):
        ref[0:BLOCK, :] = out[BLOCK * d : BLOCK * (d + 1)]
    o3[BLOCK:, LENGTH:] = jnp.zeros((16, 128), F32)
    o3[BLOCK:, 0:LENGTH] = tops[...]
    for reim in range(2):
        o3[BLOCK + reim : BLOCK + reim + 1, 0:LENGTH] -= 2.0 * TAU * (sum_a[reim, 0:1, :] + sum_b[reim, 0:1, :])


def finish_kernel(b0, b1, b2, b3, th_ref, tl_ref, kd_ref, measured, mask_ref, out_hbm, out, sems):
    row = lax.axis_index("row")
    both = second_transform(th_ref, tl_ref, (b0, b1, b2, b3), row)
    mask = SIGMA * mask_ref[...]
    scale = 1.0 / (1.0 + SIGMA / LAMBDA_DATA)
    copies = []
    for c in range(COIL):
        real = both[BLOCK * c : BLOCK * (c + 1), :LENGTH]
        imag = -both[BLOCK * c : BLOCK * (c + 1), LENGTH:]
        for plane, value in ((c, real), (COIL + c, imag)):
            out[plane] = (kd_ref[plane] + mask * (value - measured[plane])) * scale
            copies.append(pltpu.make_async_copy(out.at[plane], out_hbm.at[plane], sems.at[plane]))
            copies[-1].start()
    for copy in copies:
        copy.wait()


def along_rows(bar, plane, i):
    here = chunk(bar, plane, i)
    below = chunk(bar, plane, i + 1)
    rows = iota((8, LENGTH), 0)
    return jnp.where(rows == 7, pltpu.roll(below, 7, 0), pltpu.roll(here, 7, 0)) - here


def along_cols(bar, plane, i):
    here = chunk(bar, plane, i)
    cols = iota((8, LENGTH), 1)
    return jnp.where(cols == LENGTH - 1, 0.0, pltpu.roll(here, LENGTH - 1, 1) - here)


def project(out, duals, radius, i):
    total = duals[0] * duals[0]
    for value in duals[1:]:
        total += value * value
    scale = jnp.minimum(1.0, radius * lax.rsqrt(total))
    for plane, value in enumerate(duals):
        out[plane, 8 * i : 8 * i + 8, :] = value * scale


def by_frame(run, from_core, from_chip):
    odd = lax.rem(lax.axis_index("tm"), 2)
    pl.when(odd == 0)(lambda: run(from_chip, from_core))
    pl.when(odd == 1)(lambda: run(from_core, from_chip))


def fill_below(bar, n3, first_plane, count):
    row = lax.axis_index("row")
    for plane in range(count):
        place = BLOCK + first_plane + plane
        bar[plane, BLOCK : BLOCK + 1, :] = jnp.where(
            row == ROWS - 1, bar[plane, BLOCK - 1 : BLOCK, :], n3[place : place + 1, 0:LENGTH]
        )


def in_parts(second, pairs, copies, sems):
    for part in range(4):
        rows = pl.ds(16 * part, 16)
        second(2 * part)
        second(2 * part + 1)
        for k, (source, target) in enumerate(pairs):
            copy = pltpu.make_async_copy(source.at[:, rows, :], target.at[:, rows, :], sems.at[4 + 4 * part + k])
            copy.start()
            copies.append(copy)
    for copy in copies:
        copy.wait()


def fields_kernel(
    img, spl, v1, v2, g1, g2, s1, s2, w, q0, from_core, from_chip, z, z_in, n3,
    img_hbm, spl_hbm, v1_hbm, v2_hbm, g1_hbm, g2_hbm, s1_hbm, s2_hbm,
    bar, img_out, spl_out, v1_out, v2_out, g1_out, g2_out, s1_out, s2_out, sems,
):
    keep_time = (lax.axis_index("tm") != lax.axis_size("tm") - 1).astype(F32)
    refs = dict(g1=g1, g2=g2, s1=s1, s2=s2)

    def run(q_in, w_in):
        copies = [
            pltpu.make_async_copy(source, target, sems.at[k])
            for k, (source, target) in enumerate(
                ((img_out, img_hbm), (spl_out, spl_hbm), (v1_out, v1_hbm), (v2_out, v2_hbm))
            )
        ]

        def first(i, carry):
            for reim in range(2):

                def before(f):
                    return chunk(q0, reim, i) if f == 0 else chunk(q_in, 2 * (f - 1) + reim, i)

                values = []
                for field in range(8):
                    plane = 2 * field + reim
                    start = chunk(w, plane, i) if field else chunk(z, reim, i)
                    values.append(start + time_term(before, field))
                    bar[plane, rows_at(8 * i), :] = values[-1]
                img_out[reim, rows_at(8 * i), :] = 0.5 * (values[0] + values[1] + chunk(img, reim, i))
                spl_out[reim, rows_at(8 * i), :] = 0.5 * (values[1] + chunk(spl, reim, i))
                for k in range(3):
                    plane = 2 * k + reim
                    v1_out[plane, rows_at(8 * i), :] = 0.5 * (values[2 + k] + chunk(v1, plane, i))
                    v2_out[plane, rows_at(8 * i), :] = 0.5 * (values[5 + k] + chunk(v2, plane, i))
            return carry

        lax.fori_loop(0, 8, first, 0, unroll=2)
        for copy in copies:
            copy.start()
        fill_below(bar, n3, 0, 16)

        def along_time(field, reim, i):
            plane = 2 * field + reim

            def own(f):
                name, part = TIME_PARTS[f]
                return chunk(refs[name], 2 * part + reim, i)

            ahead = chunk(w_in, plane - 2, i) if field else chunk(z_in, reim, i)
            return ahead + time_term(own, field) - chunk(bar, plane, i)

        def second(i):
            for dual, out, field, beta in ((g1, g1_out, 0, BETA_ONE), (g2, g2_out, 1, BETA_TWO)):
                duals = []
                for k in range(3):
                    for reim in range(2):
                        if k == 0:
                            diff = (beta * keep_time) * along_time(field, reim, i)
                        else:
                            diff = (along_rows, along_cols)[k - 1](bar, 2 * field + reim, i)
                        diff -= chunk(bar, 2 * (2 + 3 * field + k) + reim, i)
                        duals.append(chunk(dual, 2 * k + reim, i) + SIGMA * diff)
                project(out, duals, ALPHA_ONE, i)
            for dual, out, vec, beta in ((s1, s1_out, 2, BETA_ONE), (s2, s2_out, 5, BETA_TWO)):
                duals = [None] * 12
                factor = SIGMA * beta * keep_time
                for reim in range(2):
                    p0, p1, p2 = (2 * (vec + k) + reim for k in range(3))
                    steps = (
                        factor * along_time(vec, reim, i),
                        SIGMA * along_rows(bar, p1, i),
                        SIGMA * along_cols(bar, p2, i),
                        0.5 * SIGMA * along_rows(bar, p0, i) + (0.5 * factor) * along_time(vec + 1, reim, i),
                        0.5 * SIGMA * along_cols(bar, p0, i) + (0.5 * factor) * along_time(vec + 2, reim, i),
                        0.5 * SIGMA * (along_cols(bar, p1, i) + along_rows(bar, p2, i)),
                    )
                    for k, diff in enumerate(steps):
                        duals[2 * k + reim] = chunk(dual, 2 * k + reim, i) + diff
                project(out, duals, ALPHA_ZERO, i)

        pairs = ((g1_out, g1_hbm), (g2_out, g2_hbm), (s1_out, s1_hbm), (s2_out, s2_hbm))
        in_parts(second, pairs, copies, sems)

    by_frame(run, from_core, from_chip)


def shape(*dims):
    return jax.ShapeDtypeStruct(dims, F32)


def call(kernel, outs, ins, cost, in_specs=None, scratch=(), out_space=pltpu.VMEM):
    return pl.pallas_call(
        kernel,
        out_shape=outs,
        in_specs=in_specs or [pl.BlockSpec(memory_space=pltpu.VMEM)] * len(ins),
        out_specs=[pl.BlockSpec(memory_space=out_space)] * len(outs),
        scratch_shapes=list(scratch),
        compiler_params=pltpu.CompilerParams(vmem_limit_bytes=LIMIT),
        cost_estimate=pl.CostEstimate(flops=500 * cost, bytes_accessed=cost, transcendentals=0),
    )(*ins)


def turn(block, distance):
    return lax.ppermute(block, "row", [(i, (i + distance) % ROWS) for i in range(ROWS)])


def body(
    image_now, split_now, vector_one, vector_two, kspace_dual, grad_one, grad_two, sym_one, sym_two,
    measured, sensitivity, sampled,
):
    planes = lambda x: x.reshape(-1, BLOCK, LENGTH)
    img, spl, v1, v2, kd = map(planes, (image_now, split_now, vector_one, vector_two, kspace_dual))
    g1, g2, s1, s2, meas, sens = map(planes, (grad_one, grad_two, sym_one, sym_two, measured, sensitivity))
    first_high, first_low, high, low = map(jnp.asarray, dft_tables())
    frames = lax.axis_size("tm")
    groups = lax.axis_size("coil")
    blocks = (shape(BLOCK, 384), shape(BLOCK + 16, 384), shape(BLOCK + 24, 384), shape(BLOCK, 384))
    hbm = pl.BlockSpec(memory_space=pltpu.HBM)
    a0, a1, a2, a3, mask = call(
        start_kernel, (*blocks, shape(1, LENGTH)),
        [pltpu.with_memory_space_constraint(x, pltpu.HBM) for x in (kd, sampled, first_high, first_low, g1, g2, s1, s2)],
        1,
        in_specs=[hbm] * 8,
        scratch=[
            pltpu.VMEM((2 * COIL, BLOCK, LENGTH), F32), pltpu.VMEM((1, LENGTH), jnp.int32),
            pltpu.VMEM((LENGTH, 2 * LENGTH), BF16), pltpu.VMEM((LENGTH, 2 * LENGTH), BF16),
            pltpu.VMEM((16, 8, LENGTH), F32), pltpu.SemaphoreType.DMA((12,)),
        ],
    )
    b2, b1, b3 = turn(a2, 2), turn(a1, 1), turn(a3, 3)
    after = [(i, i + 1) for i in range(frames - 1)]
    (q_first,) = call(
        pack_kernel, (shape(2 * BLOCK + 16, LENGTH),), (g1, g2, s1, s2, a0), 100_000_000,
        in_specs=[pl.BlockSpec(memory_space=pltpu.VMEM)] * 4 + [pl.BlockSpec(memory_space=pl.ANY)],
    )
    q_first = lax.ppermute(q_first, "tm", after)
    (partial,) = call(combine_kernel, (shape(2, BLOCK, LENGTH),), (a0, b1, b2, b3, high, low, sens), 200_000_000)
    partner = ((1, 0, 3, 2), (3, 2, 1, 0))
    swaps = [
        [(t * groups + c, t * groups + partner[(t + turn) % 2][c]) for t in range(frames) for c in range(groups)]
        for turn in range(2)
    ]
    stack, pair_of = shape(14, BLOCK, LENGTH), shape(2, BLOCK, LENGTH)
    w_out, base, tops, q0, to_core, to_chip = call(
        plain_kernel, (shape(16, BLOCK, LENGTH), pair_of, shape(16, LENGTH), pair_of, stack, stack),
        (img, spl, v1, v2, g1, g2, s1, s2, b1, q_first, partial), 100_000_000,
        in_specs=[pl.BlockSpec(memory_space=pltpu.VMEM)] * 10 + [pl.BlockSpec(memory_space=pl.ANY)],
    )
    received = lax.ppermute(partial, ("tm", "coil"), swaps[0])
    partial, received, w_out = lax.optimization_barrier((partial, received, w_out))
    pair = partial + received
    rest = lax.ppermute(pair, ("tm", "coil"), swaps[1])
    pairs = []
    for t in range(1, frames - 1, 2):
        for c in range(groups):
            there = c if t % 4 == 1 else (c + 1) % groups
            pairs.append((t * groups + c, (t + 1) * groups + there))
            pairs.append(((t + 1) * groups + there, t * groups + c))
    from_chip = lax.ppermute(to_chip, ("tm", "coil"), pairs)
    to_core, rest = lax.optimization_barrier((to_core, rest))
    from_core = lax.ppermute(to_core, "tm", [(t, t ^ 1) for t in range(frames)])
    c_blocks = (shape(BLOCK, 384), shape(BLOCK, 384), shape(BLOCK, 384), shape(BLOCK + 16, 384))
    c0, c1, c2, c3, z = call(
        predict_kernel, (*c_blocks, shape(2, BLOCK, LENGTH)),
        (pair, rest, base, tops, w_out, first_high, first_low, sens), 200_000_000,
    )
    n2, n1, n3 = turn(c2, 2), turn(c1, 1), turn(c3, 3)
    z, from_core = lax.optimization_barrier((z, from_core))
    z_in = lax.ppermute(z, "tm", [(i + 1, i) for i in range(frames - 1)])
    like = lambda x: shape(*x.shape)
    img_new, spl_new, v1_new, v2_new, g1_new, g2_new, s1_new, s2_new = call(
        fields_kernel, tuple(map(like, (img, spl, v1, v2, g1, g2, s1, s2))),
        (img, spl, v1, v2, g1, g2, s1, s2, w_out, q0, from_core, from_chip, z, z_in, n3), 1,
        scratch=[
            pltpu.VMEM((16, BLOCK + 8, LENGTH), F32),
            *(pltpu.VMEM(x.shape, F32) for x in (img, spl, v1, v2, g1, g2, s1, s2)),
            pltpu.SemaphoreType.DMA((20,)),
        ],
        out_space=pltpu.HBM,
    )
    (kspace,) = call(
        finish_kernel, (like(kd),), (c0, n1, n2, n3, high, low, kd, meas, mask), 4_000_000,
        scratch=[pltpu.VMEM(kd.shape, F32), pltpu.SemaphoreType.DMA((2 * COIL,))],
        out_space=pltpu.HBM,
    )
    news = (img_new, spl_new, v1_new, v2_new, kspace, g1_new, g2_new, s1_new, s2_new)
    olds = (image_now, split_now, vector_one, vector_two, kspace_dual, grad_one, grad_two, sym_one, sym_two)
    return tuple(new.reshape(old.shape) for new, old in zip(news, olds))


def solution(mesh):
    image = P(None, "tm", "row", None)
    vector = P(None, None, "tm", "row", None)
    kspace = P(None, "tm", "coil", "row", None)
    return jax.shard_map(
        body,
        mesh=mesh,
        in_specs=(
            image, image, vector, vector, kspace, vector, vector, vector, vector, kspace,
            P(None, "coil", "row", None), P("tm", None),
        ),
        out_specs=(image, image, vector, vector, kspace, vector, vector, vector, vector),
        check_vma=False,
    )
```
